256 devices in a mesh: ctx: 128 (over y, z, x), head: 2 (over core).
Axes of the slice: x: 4, y: 4, z: 8, core: 2. Of those that a mesh axis runs over, the one named last changes fastest.
Arguments:
- queries: bfloat16 [2, 49152, 128], P('head', 'ctx'), may hold values from -150 to 150
- keys: bfloat16 [2, 49152, 128], P('head', 'ctx'), may hold values from -8 to 8
- values: bfloat16 [2, 49152, 128], P('head', 'ctx'), may hold values from -6 to 6
- out_weight: bfloat16 [2, 128, 4096], P('head'), may hold values from -0.375 to 0.375
Outputs:
- projected: bfloat16 [49152, 4096], P('ctx', 'head')
The draws below stay inside these ranges and needn't reach their ends.
All inputs are finite; a program needn't handle non-finite values.
Results may differ from the reference program's by a relative error of at most 0.012.
Values may be sent and summed in bfloat16 or wider, within the bound.
A program may use at most 256 MiB of HBM per device.

```python
import math
import jax
import jax.numpy as jnp
from jax import lax

D = 4096
HD = 128
HEADS = 2
SEQ = 49152


def shared_rows(key):
    base_rows = jnp.clip(jax.random.normal(jax.random.fold_in(key, 11), (HEADS, SEQ, HD), jnp.float32), -6.0, 6.0)
    return base_rows


def draw_keys(key, part):
    base_rows = shared_rows(key)
    return base_rows.astype(jnp.bfloat16)


def draw_queries(key, part):
    key = jax.random.fold_in(key, 4)
    drawn_rows = 3.0 * jnp.clip(jax.random.normal(key, (HEADS, SEQ, HD), jnp.float32), -6.0, 6.0)
    return drawn_rows.astype(jnp.bfloat16)


def steps_of(own_key, extent, pieces, low, top_value):
    def one(position, blocks):
        draws = jax.random.uniform(jax.random.fold_in(jax.random.fold_in(own_key, 6), position), (blocks,), jnp.float32, low / len(pieces), top_value / len(pieces))
        return jnp.repeat(jnp.exp(draws), extent[position] // blocks).reshape((-1,) + (1,) * (len(extent) - position - 1))

    gain = one(*pieces[0])
    for cut in pieces[1:]:
        gain = gain * one(*cut)
    return gain


def centred(stream_key, shape, scale, limit, cuts=(), kind=jnp.bfloat16):
    array = jax.random.normal(stream_key, shape, jnp.float32) * scale
    if len(cuts) > 0:
        array = steps_of(stream_key, shape, cuts, -0.22, 0.18) * array
    return jnp.clip(array, min=-limit, max=limit).astype(kind)


def setup_inputs(seed: int = 0) -> dict:
    splits = jax.random.split(jax.random.key(seed), 5)
    return {
        "queries": draw_queries(jax.random.fold_in(splits[4], 71), 0),
        "keys": draw_keys(jax.random.fold_in(splits[4], 71), 0),
        "values": centred(splits[2], (HEADS, SEQ, HD), 1.0, 6.0, ((0, 2), (1, 128))),
        "out_weight": centred(splits[3], (HEADS, HD, D), (HEADS * HD) ** -0.5, 0.375, ((0, 2),)),
    }


big_negative = -1e+30
block_rows = 512

def head_attention(query_rows, key_rows, value_rows):
    scaling = 1.0 / math.sqrt(HD)
    total_rows = query_rows.shape[0]
    block_count = total_rows // block_rows
    offsets = jnp.arange(block_rows, dtype=jnp.int32)

    def one_block(block_index):
        first = (block_index * block_rows).astype(jnp.int32)
        block_queries = lax.dynamic_slice_in_dim(query_rows, first, block_rows, 0)
        query_pos = first + offsets

        def fill(key_block, buffer):
            start_key = (key_block * block_rows).astype(jnp.int32)
            block_keys = lax.dynamic_slice_in_dim(key_rows, start_key, block_rows, 0)
            scores = lax.dot_general(block_queries, block_keys, (((1,), (1,)), ((), ())), preferred_element_type=jnp.float32) * scaling
            key_pos = start_key + offsets
            scores = jnp.where(key_pos[None, :] <= query_pos[:, None], scores, jnp.float32(big_negative))
            return lax.dynamic_update_slice(buffer, scores, (jnp.int32(0), start_key))
        buffer = lax.fori_loop(0, block_index + 1, fill, jnp.full((block_rows, total_rows), big_negative, jnp.float32))
        row_max = lax.optimization_barrier(jnp.max(buffer, axis=1))

        def gather_sums(key_block, carried):
            row_total, summed = carried
            start_key = (key_block * block_rows).astype(jnp.int32)
            scores = lax.dynamic_slice_in_dim(buffer, start_key, block_rows, 1)
            block_values = lax.dynamic_slice_in_dim(value_rows, start_key, block_rows, 0)
            exps = jnp.exp(scores - row_max[:, None])
            row_total = row_total + lax.optimization_barrier(jnp.sum(exps, axis=1))
            summed = summed + jnp.dot(exps.astype(jnp.bfloat16), block_values, preferred_element_type=jnp.float32)
            return (row_total, summed)
        init = (jnp.zeros((block_rows,), jnp.float32), jnp.zeros((block_rows, HD), jnp.float32))
        row_total, summed = lax.fori_loop(0, block_index + 1, gather_sums, init)
        return (summed / row_total[:, None]).astype(jnp.bfloat16)
    blocks = lax.map(one_block, jnp.arange(block_count, dtype=jnp.int32))
    return blocks.reshape(total_rows, HD)

def reference(queries, keys, values, out_weight):
    projected = jnp.zeros((queries.shape[1], out_weight.shape[2]), jnp.float32)
    for head_index in range(queries.shape[0]):
        attention = head_attention(queries[head_index], keys[head_index], values[head_index])
        projected = projected + jnp.dot(attention, out_weight[head_index], preferred_element_type=jnp.float32)
    return projected.astype(jnp.bfloat16)
```

```python
import functools
import math

import jax
import jax.numpy as jnp
from jax import lax
from jax.experimental import pallas as pl
from jax.experimental.pallas import tpu as pltpu
from jax.sharding import PartitionSpec as P

MESH = pl.DeviceIdType.MESH
X, Y, Z = 4, 4, 8
ROWS = 384
HALF = ROWS // 2
HD = 128
KEYS = Z * HALF
SUPER = X * ROWS
TILE = 768
BLOCK = 256
SCALE2 = math.log2(math.e) / math.sqrt(HD)
LOW = -1e30
TINY = 1e-30
BF16, F32 = jnp.bfloat16, jnp.float32


def lane_rows(columns):
    parts = [columns[128 * j : 128 * (j + 1), :].T[0:1, :] for j in range(ROWS // 128)]
    return jnp.concatenate(parts, axis=0)


def lane_columns(rows):
    parts = [jnp.broadcast_to(rows[j : j + 1, :], (128, 128)).T for j in range(ROWS // 128)]
    return jnp.concatenate(parts, axis=0)


def pack_stats(rows):
    high = rows.astype(BF16).astype(F32)
    mid = (rows - high).astype(BF16).astype(F32)
    low = rows - high - mid
    return jnp.concatenate([high, mid, low, jnp.zeros((7, 128), F32)], axis=0).astype(BF16)


def unpack_stats(packed):
    wide = packed.astype(F32)
    return wide[0:3] + wide[3:6] + wide[6:9]


def merge(parts):
    top = functools.reduce(jnp.maximum, [stats for _, stats in parts])
    shares = [jnp.exp2(stats - top) for _, stats in parts]
    total = sum(shares)
    merged = None
    for (rows, _), share in zip(parts, shares):
        term = rows.astype(F32) * lane_columns(share / total)
        merged = term if merged is None else merged + term
    return merged, top + jnp.log2(total)


def attention_kernel(
    q_ref, k_ref, v_ref, w_ref, att_ref, w2_ref,
    qbuf, kvbuf, swap, kt, acc, top, obuf, r1, pbuf, r2, att, wx,
    kv_ss, kv_rs, swap_ss, q1_ss, q1_rs, q2_ss, q2_rs, o1_ss, o1_rs, o2_ss, o2_rs, c_ss, c_rs,
):
    index, core = lax.axis_index("ctx"), lax.axis_index("head")
    x, z, y = lax.rem(index, X), lax.rem(lax.div(index, X), Z), lax.div(index, X * Z)

    def at(px, py, pz, pc=None):
        return ((py * Z + pz) * X + px, core if pc is None else pc)

    def ring(p, d, n):
        return lax.rem(p + d + n, n)

    def remote(src, dst, ss, rs, where):
        return pltpu.make_async_remote_copy(
            src_ref=src, dst_ref=dst, send_sem=ss, recv_sem=rs, device_id=where, device_id_type=MESH
        )

    other = 1 - core
    up, down = at(x, y, ring(z, 1, Z)), at(x, y, ring(z, -1, Z))
    partner = at(x, y, z, other)
    x_peers = [at(ring(x, k, X), y, z) for k in range(1, X)]
    y_peers = [at(x, ring(y, k, Y), z) for k in range(1, Y)]
    first = [(jnp.where(core == 0, a[0], b[0]), core) for a, b in zip(x_peers, y_peers)]
    second = [(jnp.where(core == 0, b[0], a[0]), core) for a, b in zip(x_peers, y_peers)]
    u, v = jnp.where(core == 0, y, x), jnp.where(core == 0, x, y)

    barrier = pltpu.get_barrier_semaphore()
    for where in x_peers + y_peers + [up, down, partner]:
        pl.semaphore_signal(barrier, inc=1, device_id=where, device_id_type=MESH)
    pl.semaphore_wait(barrier, 9)

    def slot(h, s):
        return kvbuf.at[h, :, pl.ds(pl.multiple_of(s * HALF, HALF), HALF), :]

    def q_slot(n):
        return qbuf.at[n]

    own = pl.ds(pl.multiple_of(z * HALF, HALF), HALF)
    kvbuf[0, 0, own, :] = k_ref[0:HALF, :]
    kvbuf[0, 1, own, :] = v_ref[0:HALF, :]
    swap[0] = k_ref[HALF:ROWS, :]
    swap[1] = v_ref[HALF:ROWS, :]
    qbuf[u * 4 + v] = q_ref[...]

    mirror = at(x, Y - 1 - y, z)
    swap_copy = remote(swap, slot(1, z), swap_ss, kv_rs.at[1, z], mirror)
    swap_copy.start()

    def ring_copy(h, way, d):
        s = ring(z, -d if way == 0 else d, Z)
        return remote(
            slot(h, s), slot(h, s), kv_ss.at[h, way, d], kv_rs.at[h, s], up if way == 0 else down
        )

    reach = {(0, 0): 4, (0, 1): 3, (1, 0): 3, (1, 1): 4}
    sent = []

    def pass_on(h, way, d):
        if d < reach[h, way]:
            copy = ring_copy(h, way, d)
            copy.start()
            sent.append(copy)

    def arrived(h, way, d):
        if d <= reach[h, way]:
            s = ring(z, -d if way == 0 else d, Z)
            remote(slot(h, s), slot(h, s), kv_ss.at[h, way, 0], kv_rs.at[h, s], up).wait_recv()

    pass_on(0, 0, 0)
    pass_on(0, 1, 0)

    q1 = []
    for k in range(1, 4):
        copy = remote(q_slot(u * 4 + v), q_slot(u * 4 + v), q1_ss.at[k], q1_rs.at[k], first[k - 1])
        copy.start()
        q1.append(copy)
    w_copy = remote(
        w_ref.at[:, pl.ds(pl.multiple_of(other * 2048, 2048), 2048)], wx, c_ss.at[0], c_rs.at[0], partner
    )
    w_copy.start()

    remote(slot(1, z), slot(1, z), swap_ss, kv_rs.at[1, z], mirror).wait_recv()
    pass_on(1, 0, 0)
    pass_on(1, 1, 0)

    for k in range(1, 4):
        s = q_slot(u * 4 + ring(v, -k, 4))
        remote(s, s, q1_ss.at[k], q1_rs.at[k], first[k - 1]).wait_recv()
    q2 = []
    for k in range(1, 4):
        row = qbuf.at[pl.ds(u * 4, 4)]
        copy = remote(row, row, q2_ss.at[k], q2_rs.at[k], second[k - 1])
        copy.start()
        q2.append(copy)

    for d in range(1, 5):
        for h in range(2):
            for way in range(2):
                arrived(h, way, d)
                pass_on(h, way, d)
    for k in range(1, 4):
        row = qbuf.at[pl.ds(ring(u, -k, 4) * 4, 4)]
        remote(row, row, q2_ss.at[k], q2_rs.at[k], second[k - 1]).wait_recv()

    for h in range(2):
        for p in range(4):
            kt[h, :, 384 * p : 384 * (p + 1)] = kvbuf[h, 0, 384 * p : 384 * (p + 1), :].T

    def queries_of(yp, t):
        chunks = []
        for j in range(TILE // ROWS):
            xp = t * (TILE // ROWS) + j
            chunks.append(qbuf[jnp.where(core == 0, yp * 4 + xp, xp * 4 + yp)])
        return jnp.concatenate(chunks, axis=0)

    def step(state, q, keys, values, keep=None):
        old, summed = state
        score = jnp.dot(q, keys, preferred_element_type=F32)
        if keep is not None:
            score = jnp.where(keep, score, LOW)
        new = jnp.maximum(old, jnp.max(score, axis=1, keepdims=True))
        exps = jnp.exp2((score - new) * SCALE2).astype(BF16)
        both = jnp.concatenate([values, jnp.ones((BLOCK, 128), BF16)], axis=1)
        summed = summed * jnp.exp2((old - new) * SCALE2) + jnp.dot(exps, both, preferred_element_type=F32)
        return new, summed

    def load():
        return top[:, 0:1], acc[...]

    def store(state):
        top[...] = jnp.broadcast_to(state[0], (TILE, 128))
        acc[...] = state[1]

    def o1_copy(yp, k):
        xp = ring(x, k, X)
        return remote(obuf.at[yp, xp], r1.at[yp, x], o1_ss.at[yp, k], o1_rs.at[yp, k], at(xp, y, z))

    def o2_copy(yp):
        return remote(pbuf.at[yp], r2.at[y], o2_ss.at[yp], o2_rs.at[y], at(x, yp, z))

    def one_super(yp, _):
        def one_tile(t, _):
            acc[...] = jnp.zeros_like(acc)
            top[...] = jnp.full_like(top, LOW)
            q = queries_of(yp, t)

            def one_group(h, _):
                ky = jnp.where(h == 0, y, Y - 1 - y)

                @pl.when(yp > ky)
                def _():
                    state = load()
                    for b in range(KEYS // BLOCK):
                        span = slice(b * BLOCK, (b + 1) * BLOCK)
                        state = step(state, q, kt[h, :, span], kvbuf[h, 1, span, :])
                    store(state)

                @pl.when(yp == ky)
                def _():
                    count = lax.div(HALF * z + HALF - 1, BLOCK) + 1
                    query = t * TILE + z * SUPER + lax.broadcasted_iota(jnp.int32, (TILE, BLOCK), 0)

                    def masked(b, _):
                        span = pl.ds(pl.multiple_of(b * BLOCK, BLOCK), BLOCK)
                        n = b * BLOCK + lax.broadcasted_iota(jnp.int32, (1, BLOCK), 1)
                        place = n + (x * ROWS + h * HALF)
                        for edge in range(1, Z):
                            place = place + jnp.where(n >= edge * HALF, SUPER - HALF, 0)
                        store(step(load(), q, kt[h, :, span], kvbuf[h, 1, span, :], place <= query))
                        return 0

                    lax.fori_loop(0, count, masked, 0)

                return 0

            lax.fori_loop(0, 2, one_group, 0)
            for j in range(TILE // ROWS):
                span = slice(j * ROWS, (j + 1) * ROWS)
                total = jnp.maximum(acc[span, 128:256], TINY)
                xp = t * (TILE // ROWS) + j
                obuf[yp, xp, 0:ROWS, :] = (acc[span, 0:128] / total).astype(BF16)
                stats = top[span, :] * SCALE2 + jnp.log2(total)
                obuf[yp, xp, ROWS : ROWS + 16, :] = pack_stats(lane_rows(stats))
            return 0

        lax.fori_loop(0, SUPER // TILE, one_tile, 0)
        for k in range(1, 4):
            o1_copy(yp, k).start()
        r1[yp, x] = obuf[yp, x]
        return 0

    lax.fori_loop(0, Y, one_super, 0)

    def read(ref):
        return ref[0:ROWS, :], unpack_stats(ref[ROWS : ROWS + 16, :])

    def first_merge(yp, _):
        for k in range(1, 4):
            s = r1.at[yp, ring(x, -k, X)]
            remote(s, s, o1_ss.at[yp, k], o1_rs.at[yp, k], partner).wait_recv()
        merged, stats = merge([read(r1.at[yp, s]) for s in range(4)])
        pbuf[yp, 0:ROWS, :] = merged.astype(BF16)
        pbuf[yp, ROWS : ROWS + 16, :] = pack_stats(stats)

        @pl.when(yp != y)
        def _():
            o2_copy(yp).start()

        @pl.when(yp == y)
        def _():
            r2[y] = pbuf[yp]

        return 0

    lax.fori_loop(0, Y, first_merge, 0)

    for k in range(1, 4):
        s = ring(y, k, Y)
        remote(r2.at[s], r2.at[s], o2_ss.at[0], o2_rs.at[s], partner).wait_recv()
    merged, _ = merge([read(r2.at[s]) for s in range(4)])
    att[core] = merged.astype(BF16)
    att_copy = remote(att.at[core], att.at[core], c_ss.at[1], c_rs.at[1], partner)
    att_copy.start()

    swap_copy.wait_send()
    for copy in sent + q1 + q2:
        copy.wait_send()

    def drain(yp, _):
        for k in range(1, 4):
            o1_copy(yp, k).wait_send()

        @pl.when(yp != y)
        def _():
            o2_copy(yp).wait_send()

        return 0

    lax.fori_loop(0, Y, drain, 0)
    w_copy.wait()
    w2_ref[core] = w_ref[:, pl.ds(pl.multiple_of(core * 2048, 2048), 2048)]
    w2_ref[other] = wx[...]
    att_copy.wait_send()
    remote(att.at[other], att.at[other], c_ss.at[1], c_rs.at[1], partner).wait_recv()
    att_ref[...] = att[...]


def project_kernel(att_ref, w_ref, out_ref):
    out_ref[...] = (
        jnp.dot(att_ref[0], w_ref[0], preferred_element_type=F32)
        + jnp.dot(att_ref[1], w_ref[1], preferred_element_type=F32)
    ).astype(BF16)


def per_device(queries, keys, values, out_weight):
    vmem = pl.BlockSpec(memory_space=pltpu.VMEM)
    dma = pltpu.SemaphoreType.DMA
    att, w2 = pl.pallas_call(
        attention_kernel,
        out_shape=(
            jax.ShapeDtypeStruct((2, ROWS, HD), BF16),
            jax.ShapeDtypeStruct((2, HD, 2048), BF16),
        ),
        in_specs=[vmem] * 4,
        out_specs=(vmem, vmem),
        scratch_shapes=[
            pltpu.VMEM((16, ROWS, HD), BF16),
            pltpu.VMEM((2, 2, KEYS, HD), BF16),
            pltpu.VMEM((2, HALF, HD), BF16),
            pltpu.VMEM((2, HD, KEYS), BF16),
            pltpu.VMEM((TILE, 256), F32),
            pltpu.VMEM((TILE, 128), F32),
            pltpu.VMEM((4, 4, ROWS + 16, HD), BF16),
            pltpu.VMEM((4, 4, ROWS + 16, HD), BF16),
            pltpu.VMEM((4, ROWS + 16, HD), BF16),
            pltpu.VMEM((4, ROWS + 16, HD), BF16),
            pltpu.VMEM((2, ROWS, HD), BF16),
            pltpu.VMEM((HD, 2048), BF16),
            dma((2, 2, 4)), dma((2, 8)), dma, dma((4,)), dma((4,)), dma((4,)), dma((4,)),
            dma((4, 4)), dma((4, 4)), dma((4,)), dma((4,)), dma((2,)), dma((2,)),
        ],
        compiler_params=pltpu.CompilerParams(
            collective_id=0, has_side_effects=True, vmem_limit_bytes=50 << 20
        ),
    )(queries[0], keys[0], values[0], out_weight[0])
    return pl.pallas_call(
        project_kernel,
        grid=(4,),
        out_shape=jax.ShapeDtypeStruct((ROWS, 2048), BF16),
        in_specs=[
            pl.BlockSpec((2, ROWS, HD), lambda n: (0, 0, 0)),
            pl.BlockSpec((2, HD, 512), lambda n: (0, 0, n)),
        ],
        out_specs=pl.BlockSpec((ROWS, 512), lambda n: (0, n)),
    )(att, w2)


def solution(mesh):
    placed = (
        P("head", "ctx", None),
        P("head", "ctx", None),
        P("head", "ctx", None),
        P("head", None, None),
    )
    return jax.shard_map(
        per_device, mesh=mesh, in_specs=placed, out_specs=P("ctx", "head"), check_vma=False
    )
```

```python
import functools
import math

import jax
import jax.numpy as jnp
from jax import lax
from jax.experimental import pallas as pl
from jax.experimental.pallas import tpu as pltpu
from jax.sharding import PartitionSpec as P

MESH = pl.DeviceIdType.MESH
X, Y, Z = 4, 4, 8
ROWS = 384
HALF = ROWS // 2
HD = 128
LINE = Z * HALF
SUPER = X * ROWS
TILE = LINE // 2
BLOCK = 256
WIDTH = 2048
MESSAGE = HALF + 16
SCALE2 = math.log2(math.e) / math.sqrt(HD)
LOW = -1e30
TINY = 1e-30
BF16, F32 = jnp.bfloat16, jnp.float32


def lane_rows(columns):
    return jnp.concatenate([columns[0:128].T[0:1], columns[HALF - 128 : HALF].T[0:1]], axis=0)


def lane_columns(rows):
    low = jnp.broadcast_to(rows[0:1], (128, 128)).T
    high = jnp.broadcast_to(rows[1:2], (128, 128)).T
    return jnp.concatenate([low, high[256 - HALF : 128]], axis=0)


def pack_stats(rows):
    high = rows.astype(BF16).astype(F32)
    mid = (rows - high).astype(BF16).astype(F32)
    low = rows - high - mid
    return jnp.concatenate([high, mid, low, jnp.zeros((10, 128), F32)], axis=0).astype(BF16)


def unpack_stats(packed):
    wide = packed.astype(F32)
    return wide[0:2] + wide[2:4] + wide[4:6]


def attention_kernel(
    q_ref, k_ref, v_ref, w_ref, out_ref,
    qbuf, kvbuf, kt, swap, acc, top, obuf, rbuf, att, w2, proj,
    in_s, kv1_ss, kv2_ss, kv_rs, swap_ss, q_ss, q_rs, o_ss, o_rs, c_ss, c_rs, out_s,
):
    index, core = lax.axis_index("ctx"), lax.axis_index("head")
    x, z, y = lax.rem(index, X), lax.rem(lax.div(index, X), Z), lax.div(index, X * Z)
    ym = Y - 1 - y

    def at(px, py, pz, pc=None):
        return ((py * Z + pz) * X + px, core if pc is None else pc)

    def ring(p, d, n):
        return lax.rem(p + d + n, n)

    def remote(src, dst, ss, rs, where):
        return pltpu.make_async_remote_copy(
            src_ref=src, dst_ref=dst, send_sem=ss, recv_sem=rs, device_id=where, device_id_type=MESH
        )

    other = 1 - core
    partner = at(x, y, z, other)
    x_peers = [at(ring(x, k, X), y, z) for k in range(1, X)]
    y_peers = [at(x, ring(y, k, Y), z) for k in range(1, Y)]
    lines = [[at(x, yy, ring(z, k, Z)) for k in range(Z)] for yy in (y, ym)]
    first = [(jnp.where(core == 0, a[0], b[0]), core) for a, b in zip(x_peers, y_peers)]
    second = [(jnp.where(core == 0, b[0], a[0]), core) for a, b in zip(x_peers, y_peers)]

    def rows_at(n, size):
        return pl.ds(pl.multiple_of(n * size, size), size)

    def chunk(n):
        return kvbuf.at[:, rows_at(n, ROWS), :]

    mine = y * X + x
    loads = [
        pltpu.make_async_copy(k_ref, kvbuf.at[0, rows_at(mine, ROWS)], in_s.at[0]),
        pltpu.make_async_copy(v_ref, kvbuf.at[1, rows_at(mine, ROWS)], in_s.at[1]),
        pltpu.make_async_copy(q_ref.at[0:HALF], qbuf.at[0, rows_at(z, HALF)], in_s.at[2]),
        pltpu.make_async_copy(q_ref.at[HALF:ROWS], swap, in_s.at[3]),
        pltpu.make_async_copy(
            w_ref.at[:, rows_at(core, WIDTH)], w2.at[rows_at(core, HD)], in_s.at[4]
        ),
    ]
    for copy in loads:
        copy.start()

    barrier = pltpu.get_barrier_semaphore()
    for where in lines[0][1:] + lines[1] + x_peers + y_peers + [partner]:
        pl.semaphore_signal(barrier, inc=1, device_id=where, device_id_type=MESH)
    pl.semaphore_wait(barrier, 22)

    sent = []

    def send(copy):
        copy.start()
        sent.append(copy)

    for copy in loads[:4]:
        copy.wait()
    for k in (1, 3, 2):
        send(remote(chunk(mine), chunk(mine), kv1_ss.at[k], kv_rs.at[mine], first[k - 1]))
    own_rows = [qbuf.at[h, rows_at(z, HALF)] for h in range(2)]
    send(remote(swap, own_rows[1], swap_ss, q_rs.at[1, z], lines[1][0]))
    for k in (1, 7, 2, 6, 3, 5, 4):
        send(remote(own_rows[0], own_rows[0], q_ss.at[0, k], q_rs.at[0, z], lines[0][k]))
    for k in (1, 3, 2):
        send(remote(chunk(mine), chunk(mine), kv2_ss.at[0, k], kv_rs.at[mine], second[k - 1]))
    remote(own_rows[1], own_rows[1], swap_ss, q_rs.at[1, z], partner).wait_recv()
    for k in (1, 7, 2, 6, 3, 5, 4):
        send(remote(own_rows[1], own_rows[1], q_ss.at[1, k], q_rs.at[1, z], lines[0][k]))
    send(
        remote(
            w_ref.at[:, rows_at(other, WIDTH)], w2.at[rows_at(core, HD)], c_ss.at[0], c_rs.at[0], partner
        )
    )

    def clear(n, _):
        acc[n] = jnp.zeros((LINE, 256), F32)
        top[n] = jnp.full((LINE, 128), LOW, F32)
        return 0

    lax.fori_loop(0, 2, clear, 0)

    for j in (1, 3, 2):
        n = jnp.where(core == 0, y * X + ring(x, -j, X), ring(y, -j, Y) * X + x)
        remote(chunk(n), chunk(n), kv1_ss.at[j], kv_rs.at[n], partner).wait_recv()
        for k in (1, 3, 2):
            send(remote(chunk(n), chunk(n), kv2_ss.at[j, k], kv_rs.at[n], second[k - 1]))

    def step(state, q, keys, values, keep=None):
        old, summed = state
        score = jnp.dot(q, keys, preferred_element_type=F32)
        if keep is not None:
            score = jnp.where(keep, score, LOW)
        new = jnp.maximum(old, jnp.max(score, axis=1, keepdims=True))
        exps = jnp.exp2((score - new) * SCALE2).astype(BF16)
        both = jnp.concatenate([values, jnp.ones(values.shape, BF16)], axis=1)
        summed = summed * jnp.exp2((old - new) * SCALE2) + jnp.dot(exps, both, preferred_element_type=F32)
        return new, summed

    def attend(h, start, count, yp, limit=None):
        span = pl.ds(pl.multiple_of(start, count), count)
        q = qbuf[h, span, :]
        state = top[h, span, 0:1], acc[h, span, :]
        for b in range(SUPER // BLOCK):
            values = kvbuf[1, pl.ds(pl.multiple_of(yp * SUPER + b * BLOCK, BLOCK), BLOCK), :]
            keep = None
            if limit is not None:
                keep = b * BLOCK + lax.broadcasted_iota(jnp.int32, (count, BLOCK), 1) <= limit
            state = step(state, q, kt[yp, :, b * BLOCK : (b + 1) * BLOCK], values, keep)
        top[h, span, :] = jnp.broadcast_to(state[0], (count, 128))
        acc[h, span, :] = state[1]

    def task(h, g, yp):
        yq = jnp.where(h == 0, y, ym)

        @pl.when(yp < yq)
        def _():
            attend(h, g * TILE, TILE, yp)

        @pl.when(yp == yq)
        def _():
            edge = lax.div(z, 2)

            def pair(i, _):
                @pl.when(i > edge)
                def _():
                    attend(h, i * ROWS, ROWS, yp)

                @pl.when(i == edge)
                def _():
                    row = lax.broadcasted_iota(jnp.int32, (ROWS, 1), 0)
                    here = row + (x * ROWS + h * HALF)
                    low = jnp.where(lax.rem(z, 2) == 0, here, -1)
                    high = jnp.where(lax.rem(z, 2) == 0, SUPER, here - HALF)
                    attend(h, i * ROWS, ROWS, yp, jnp.where(row < HALF, low, high))

                return 0

            lax.fori_loop(2 * g, 2 * g + 2, pair, 0)

    def need_keys(yp):
        for xp in range(X):
            n = yp * X + xp

            @pl.when(jnp.where(core == 0, yp != y, x != xp))
            def _():
                remote(chunk(n), chunk(n), kv1_ss.at[0], kv_rs.at[n], partner).wait_recv()

        for p in range(4):
            rows = pl.ds(pl.multiple_of(yp * SUPER + ROWS * p, ROWS), ROWS)
            kt[yp, :, ROWS * p : ROWS * (p + 1)] = kvbuf[0, rows, :].T

    def need_queries(h, g):
        for t in range(4):
            s = 4 * g + t

            @pl.when(s != z)
            def _():
                r = qbuf.at[h, rows_at(s, HALF)]
                remote(r, r, q_ss.at[0, 0], q_rs.at[h, s], partner).wait_recv()

    def o_copy(h, s):
        where = at(x, jnp.where(h == 0, y, ym), s)
        return remote(obuf.at[h, s], rbuf.at[h, z], o_ss.at[h, s], o_rs.at[h, z], where)

    def finish(h, g):
        def one(t, _):
            s = 4 * g + t
            span = rows_at(s, HALF)
            total = jnp.maximum(acc[h, span, 128:256], TINY)
            obuf[h, s, 0:HALF, :] = (acc[h, span, 0:128] / total).astype(BF16)
            stats = top[h, span, :] * SCALE2 + jnp.log2(total)
            obuf[h, s, HALF:MESSAGE, :] = pack_stats(lane_rows(stats))

            @pl.when((h == 1) | (s != z))
            def _():
                o_copy(h, s).start()

            @pl.when((h == 0) & (s == z))
            def _():
                rbuf[0, z] = obuf[0, z]

            return 0

        lax.fori_loop(0, 4, one, 0)

    def superblock(e):
        return ring(y, jnp.where(e == 0, 0, jnp.where(e == 1, 3, e - 1)), Y)

    near = lax.div(z, 4)

    def work(i, _):
        early = i < 8
        late = i - 8
        e = jnp.where(early, lax.div(i, 4), 2 + lax.rem(i, 2))
        j = jnp.where(early, 3 - lax.rem(i, 4), lax.div(late, 2))
        h = 1 - lax.div(j, 2)
        g = jnp.where(lax.rem(j, 2) == 0, 1 - near, near)
        yp = superblock(e)

        @pl.when((early & (lax.rem(i, 4) == 0)) | (i == 8) | (i == 9))
        def _():
            need_keys(yp)

        @pl.when(i < 4)
        def _():
            need_queries(h, g)

        task(h, g, yp)

        @pl.when((i > 8) & (lax.rem(i, 2) == 1))
        def _():
            finish(h, g)

        return 0

    lax.fori_loop(0, 16, work, 0)

    def merge(h, _):
        for s in range(Z):

            @pl.when((h == 1) | (z != s))
            def _():
                remote(rbuf.at[h, s], rbuf.at[h, s], o_ss.at[0, 0], o_rs.at[h, s], partner).wait_recv()

        stats = [unpack_stats(rbuf[h, s, HALF:MESSAGE, :]) for s in range(Z)]
        highest = functools.reduce(jnp.maximum, stats)
        shares = [jnp.exp2(one - highest) for one in stats]
        total = functools.reduce(jnp.add, shares)
        merged = jnp.zeros((HALF, HD), F32)
        for s in range(Z):
            merged = merged + rbuf[h, s, 0:HALF, :].astype(F32) * lane_columns(shares[s] / total)
        att[core, rows_at(h, HALF), :] = merged.astype(BF16)
        return 0

    lax.fori_loop(0, 2, merge, 0)
    att_copy = remote(att.at[core], att.at[core], c_ss.at[1], c_rs.at[1], partner)
    att_copy.start()

    for copy in sent:
        copy.wait_send()

    def drain(s, _):
        for h in range(2):

            @pl.when((h == 1) | (s != z))
            def _():
                o_copy(h, s).wait_send()

        return 0

    lax.fori_loop(0, Z, drain, 0)
    loads[4].wait()
    w_other = w2.at[rows_at(other, HD)]
    remote(w_other, w_other, c_ss.at[0], c_rs.at[0], partner).wait_recv()
    att_copy.wait_send()
    remote(att.at[other], att.at[other], c_ss.at[1], c_rs.at[1], partner).wait_recv()
    both = jnp.concatenate([att[0], att[1]], axis=1)
    outs = []
    for n in range(4):
        span = slice(n * 512, (n + 1) * 512)
        proj[:, span] = jnp.dot(both, w2[:, span], preferred_element_type=F32).astype(BF16)
        copy = pltpu.make_async_copy(proj.at[:, span], out_ref.at[:, span], out_s.at[n])
        copy.start()
        outs.append(copy)
    for copy in outs:
        copy.wait()


def per_device(queries, keys, values, out_weight):
    hbm = pl.BlockSpec(memory_space=pl.ANY)
    dma = pltpu.SemaphoreType.DMA
    return pl.pallas_call(
        attention_kernel,
        out_shape=jax.ShapeDtypeStruct((ROWS, WIDTH), BF16),
        in_specs=[hbm] * 4,
        out_specs=hbm,
        scratch_shapes=[
            pltpu.VMEM((2, LINE, HD), BF16),
            pltpu.VMEM((2, Y * SUPER, HD), BF16),
            pltpu.VMEM((Y, HD, SUPER), BF16),
            pltpu.VMEM((HALF, HD), BF16),
            pltpu.VMEM((2, LINE, 256), F32),
            pltpu.VMEM((2, LINE, 128), F32),
            pltpu.VMEM((2, Z, MESSAGE, HD), BF16),
            pltpu.VMEM((2, Z, MESSAGE, HD), BF16),
            pltpu.VMEM((2, ROWS, HD), BF16),
            pltpu.VMEM((2 * HD, WIDTH), BF16),
            pltpu.VMEM((ROWS, WIDTH), BF16),
            dma((5,)), dma((4,)), dma((4, 4)), dma((16,)), dma, dma((2, 8)), dma((2, 8)), dma((2, 8)), dma((2, 8)),
            dma((2,)), dma((2,)), dma((4,)),
        ],
        compiler_params=pltpu.CompilerParams(
            collective_id=0, has_side_effects=True, vmem_limit_bytes=56 << 20
        ),
    )(queries[0], keys[0], values[0], out_weight[0])


def solution(mesh):
    placed = (
        P("head", "ctx", None),
        P("head", "ctx", None),
        P("head", "ctx", None),
        P("head", None, None),
    )
    return jax.shard_map(
        per_device, mesh=mesh, in_specs=placed, out_specs=P("ctx", "head"), check_vma=False
    )
```

```python
import functools
import math

import jax
import jax.numpy as jnp
from jax import lax
from jax.experimental import pallas as pl
from jax.experimental.pallas import tpu as pltpu
from jax.sharding import PartitionSpec as P

MESH = pl.DeviceIdType.MESH
X, Y, Z = 4, 4, 8
ROWS = 384
HALF = ROWS // 2
HD = 128
LINE = Z * HALF
SUPER = X * ROWS
TILE = LINE // 2
BLOCK = 512
WIDTH = 2048
MESSAGE = HALF + 16
SCALE2 = math.log2(math.e) / math.sqrt(HD)
LOW = -1e30
TINY = 1e-30
BF16, F32 = jnp.bfloat16, jnp.float32


def lane_rows(columns):
    return jnp.concatenate([columns[0:128].T[0:1], columns[HALF - 128 : HALF].T[0:1]], axis=0)


def lane_columns(rows):
    low = jnp.broadcast_to(rows[0:1], (128, 128)).T
    high = jnp.broadcast_to(rows[1:2], (128, 128)).T
    return jnp.concatenate([low, high[256 - HALF : 128]], axis=0)


def pack_stats(rows):
    high = rows.astype(BF16).astype(F32)
    mid = (rows - high).astype(BF16).astype(F32)
    low = rows - high - mid
    return jnp.concatenate([high, mid, low, jnp.zeros((10, 128), F32)], axis=0).astype(BF16)


def unpack_stats(packed):
    wide = packed.astype(F32)
    return wide[0:2] + wide[2:4] + wide[4:6]


def attention_kernel(
    q_ref, k_ref, v_ref, w_ref, out_ref,
    qbuf, kvbuf, kt, swap, acc, top, obuf, rbuf, att, w2, proj,
    in_s, kv1_ss, kv2_ss, kv_rs, swap_ss, q_ss, q_rs, o_ss, o_rs, c_ss, c_rs, out_s,
):
    index, core = lax.axis_index("ctx"), lax.axis_index("head")
    x, z, y = lax.rem(index, X), lax.rem(lax.div(index, X), Z), lax.div(index, X * Z)
    ym = Y - 1 - y
    near = lax.div(z, 4)

    def at(px, py, pz, pc=None):
        return ((py * Z + pz) * X + px, core if pc is None else pc)

    def ring(p, d, n):
        return lax.rem(p + d + n, n)

    def remote(src, dst, ss, rs, where):
        return pltpu.make_async_remote_copy(
            src_ref=src, dst_ref=dst, send_sem=ss, recv_sem=rs, device_id=where, device_id_type=MESH
        )

    other = 1 - core
    partner = at(x, y, z, other)
    x_peers = [at(ring(x, k, X), y, z) for k in range(1, X)]
    y_peers = [at(x, ring(y, k, Y), z) for k in range(1, Y)]
    lines = [[at(x, yy, ring(z, k, Z)) for k in range(Z)] for yy in (y, ym)]
    first = [(jnp.where(core == 0, a[0], b[0]), core) for a, b in zip(x_peers, y_peers)]
    second = [(jnp.where(core == 0, b[0], a[0]), core) for a, b in zip(x_peers, y_peers)]

    def rows_at(n, size):
        return pl.ds(pl.multiple_of(n * size, size), size)

    def chunk(n):
        return kvbuf.at[:, rows_at(n, ROWS), :]

    mine = y * X + x
    loads = [
        pltpu.make_async_copy(k_ref, kvbuf.at[0, rows_at(mine, ROWS)], in_s.at[0]),
        pltpu.make_async_copy(v_ref, kvbuf.at[1, rows_at(mine, ROWS)], in_s.at[1]),
        pltpu.make_async_copy(q_ref.at[0:HALF], qbuf.at[0, rows_at(z, HALF)], in_s.at[2]),
        pltpu.make_async_copy(q_ref.at[HALF:ROWS], swap, in_s.at[3]),
        pltpu.make_async_copy(
            w_ref.at[:, rows_at(core, WIDTH)], w2.at[rows_at(core, HD)], in_s.at[4]
        ),
    ]
    for copy in loads:
        copy.start()

    barrier = pltpu.get_barrier_semaphore()
    for where in lines[0][1:] + lines[1] + x_peers + y_peers + [partner]:
        pl.semaphore_signal(barrier, inc=1, device_id=where, device_id_type=MESH)
    pl.semaphore_wait(barrier, 22)

    sent = []

    def send(copy):
        copy.start()
        sent.append(copy)

    for copy in loads[:4]:
        copy.wait()
    for k in (1, 3, 2):
        send(remote(chunk(mine), chunk(mine), kv1_ss.at[k], kv_rs.at[mine], first[k - 1]))
    own_rows = [qbuf.at[h, rows_at(z, HALF)] for h in range(2)]
    send(remote(swap, own_rows[1], swap_ss, q_rs.at[1, z], lines[1][0]))
    for k in (1, 7, 2, 6, 3, 5, 4):
        send(remote(own_rows[0], own_rows[0], q_ss.at[0, k], q_rs.at[0, z], lines[0][k]))
    for k in (1, 3, 2):
        send(remote(chunk(mine), chunk(mine), kv2_ss.at[0, k], kv_rs.at[mine], second[k - 1]))
    remote(own_rows[1], own_rows[1], swap_ss, q_rs.at[1, z], partner).wait_recv()
    for k in (1, 7, 2, 6, 3, 5, 4):
        send(remote(own_rows[1], own_rows[1], q_ss.at[1, k], q_rs.at[1, z], lines[0][k]))
    send(
        remote(
            w_ref.at[:, rows_at(other, WIDTH)], w2.at[rows_at(core, HD)], c_ss.at[0], c_rs.at[0], partner
        )
    )

    def clear(n, _):
        acc[n] = jnp.zeros((LINE, 256), F32)
        top[n] = jnp.full((LINE, 128), LOW, F32)
        return 0

    lax.fori_loop(0, 2, clear, 0)

    for j in (1, 3, 2):
        n = jnp.where(core == 0, y * X + ring(x, -j, X), ring(y, -j, Y) * X + x)
        remote(chunk(n), chunk(n), kv1_ss.at[j], kv_rs.at[n], partner).wait_recv()
        for k in (1, 3, 2):
            send(remote(chunk(n), chunk(n), kv2_ss.at[j, k], kv_rs.at[n], second[k - 1]))

    def spread(parts):
        highest = jnp.max(functools.reduce(jnp.maximum, parts), axis=1, keepdims=True)
        return jnp.broadcast_to(highest, parts[0].shape)

    def twice(a):
        return jnp.concatenate([a, a], axis=1)

    def weigh(pieces, new):
        return jnp.concatenate([jnp.exp2((one - new) * SCALE2).astype(BF16) for one in pieces], axis=1)

    def score(h, span, yp, b):
        keys = kt[yp, :, b * BLOCK : (b + 1) * BLOCK]
        both = jnp.dot(qbuf[h, span, :], keys, preferred_element_type=F32)
        return [both[:, n * 128 : (n + 1) * 128] for n in range(BLOCK // 128)]

    def values_of(yp, start, count):
        values = kvbuf[1, pl.ds(pl.multiple_of(yp * SUPER + start, BLOCK), count), :]
        return jnp.concatenate([values, jnp.ones(values.shape, BF16)], axis=1)

    def attend(h, g, yp):
        spans = [pl.ds(pl.multiple_of(g * TILE + t * ROWS, ROWS), ROWS) for t in range(TILE // ROWS)]

        def scores(span):
            return [piece for b in range(SUPER // BLOCK) for piece in score(h, span, yp, b)]

        pieces = scores(spans[0])
        for t, span in enumerate(spans):
            later = scores(spans[t + 1]) if t + 1 < len(spans) else None
            old = top[h, span, :]
            new = jnp.maximum(old, spread(pieces))
            added = jnp.dot(weigh(pieces, new), values_of(yp, 0, SUPER), preferred_element_type=F32)
            acc[h, span, :] = acc[h, span, :] * twice(jnp.exp2((old - new) * SCALE2)) + added
            top[h, span, :] = new
            pieces = later

    def attend_below(h, i, yp, limit):
        span = pl.ds(pl.multiple_of(i * ROWS, ROWS), ROWS)
        lane = lax.broadcasted_iota(jnp.int32, (ROWS, 128), 1)

        def kept(b):
            pieces = score(h, span, yp, b)
            return [
                jnp.where(lane + (b * BLOCK + n * 128) <= limit, one, LOW) for n, one in enumerate(pieces)
            ]

        old, summed = top[h, span, :], acc[h, span, :]
        pieces = kept(0)
        for b in range(SUPER // BLOCK):
            later = kept(b + 1) if b + 1 < SUPER // BLOCK else None
            new = jnp.maximum(old, spread(pieces))
            added = jnp.dot(
                weigh(pieces, new), values_of(yp, b * BLOCK, BLOCK), preferred_element_type=F32
            )
            summed = summed * twice(jnp.exp2((old - new) * SCALE2)) + added
            old, pieces = new, later
        top[h, span, :] = old
        acc[h, span, :] = summed

    def task(h, g, yp):
        yq = jnp.where(h == 0, y, ym)

        @pl.when((yp < yq) | ((yp == yq) & (g > near)))
        def _():
            attend(h, g, yp)

        @pl.when((yp == yq) & (g == near))
        def _():
            edge = lax.div(z, 2)

            def pair(i, _):
                row = lax.broadcasted_iota(jnp.int32, (ROWS, 128), 0)
                here = row + (x * ROWS + h * HALF)
                even = lax.rem(z, 2) == 0
                low = jnp.where(even, here, -1)
                high = jnp.where(even, SUPER, here - HALF)
                limit = jnp.where(row < HALF, low, high)
                attend_below(h, i, yp, jnp.where(i > edge, SUPER, limit))
                return 0

            lax.fori_loop(edge, 2 * g + 2, pair, 0)

    def need_keys(yp):
        for xp in range(X):
            n = yp * X + xp

            @pl.when(jnp.where(core == 0, yp != y, x != xp))
            def _():
                remote(chunk(n), chunk(n), kv1_ss.at[0], kv_rs.at[n], partner).wait_recv()

        for p in range(4):
            rows = pl.ds(pl.multiple_of(yp * SUPER + ROWS * p, ROWS), ROWS)
            kt[yp, :, ROWS * p : ROWS * (p + 1)] = kvbuf[0, rows, :].T

    def need_queries(h, g):
        for t in range(4):
            s = 4 * g + t

            @pl.when(s != z)
            def _():
                r = qbuf.at[h, rows_at(s, HALF)]
                remote(r, r, q_ss.at[0, 0], q_rs.at[h, s], partner).wait_recv()

    def o_copy(h, s):
        where = at(x, jnp.where(h == 0, y, ym), s)
        return remote(obuf.at[h, s], rbuf.at[h, z], o_ss.at[h, s], o_rs.at[h, z], where)

    def finish(h, g):
        def one(t, _):
            s = 4 * g + t
            span = rows_at(s, HALF)
            total = jnp.maximum(acc[h, span, 128:256], TINY)
            obuf[h, s, 0:HALF, :] = (acc[h, span, 0:128] / total).astype(BF16)
            stats = top[h, span, :] * SCALE2 + jnp.log2(total)
            obuf[h, s, HALF:MESSAGE, :] = pack_stats(lane_rows(stats))

            @pl.when((h == 1) | (s != z))
            def _():
                o_copy(h, s).start()

            @pl.when((h == 0) & (s == z))
            def _():
                rbuf[0, z] = obuf[0, z]

            return 0

        lax.fori_loop(0, 4, one, 0)

    def superblock(e):
        return ring(y, jnp.where(e == 0, 0, jnp.where(e == 1, 3, e - 1)), Y)

    def work(i, _):
        early = i < 8
        late = i - 8
        e = jnp.where(early, lax.div(i, 4), 2 + lax.rem(i, 2))
        j = jnp.where(early, 3 - lax.rem(i, 4), lax.div(late, 2))
        h = 1 - lax.div(j, 2)
        g = jnp.where(lax.rem(j, 2) == 0, 1 - near, near)
        yp = superblock(e)

        @pl.when((early & (lax.rem(i, 4) == 0)) | (i == 8) | (i == 9))
        def _():
            need_keys(yp)

        @pl.when(i < 4)
        def _():
            need_queries(h, g)

        task(h, g, yp)

        @pl.when((i > 8) & (lax.rem(i, 2) == 1))
        def _():
            finish(h, g)

        return 0

    lax.fori_loop(0, 16, work, 0)

    def merge(h, _):
        for s in range(Z):

            @pl.when((h == 1) | (z != s))
            def _():
                remote(rbuf.at[h, s], rbuf.at[h, s], o_ss.at[0, 0], o_rs.at[h, s], partner).wait_recv()

        stats = [unpack_stats(rbuf[h, s, HALF:MESSAGE, :]) for s in range(Z)]
        highest = functools.reduce(jnp.maximum, stats)
        shares = [jnp.exp2(one - highest) for one in stats]
        total = functools.reduce(jnp.add, shares)
        merged = jnp.zeros((HALF, HD), F32)
        for s in range(Z):
            merged = merged + rbuf[h, s, 0:HALF, :].astype(F32) * lane_columns(shares[s] / total)
        att[core, rows_at(h, HALF), :] = merged.astype(BF16)
        return 0

    lax.fori_loop(0, 2, merge, 0)
    att_copy = remote(att.at[core], att.at[core], c_ss.at[1], c_rs.at[1], partner)
    att_copy.start()

    for copy in sent:
        copy.wait_send()

    def drain(s, _):
        for h in range(2):

            @pl.when((h == 1) | (s != z))
            def _():
                o_copy(h, s).wait_send()

        return 0

    lax.fori_loop(0, Z, drain, 0)
    loads[4].wait()
    w_other = w2.at[rows_at(other, HD)]
    remote(w_other, w_other, c_ss.at[0], c_rs.at[0], partner).wait_recv()
    att_copy.wait_send()
    remote(att.at[other], att.at[other], c_ss.at[1], c_rs.at[1], partner).wait_recv()
    both = jnp.concatenate([att[0], att[1]], axis=1)
    outs = []
    for n in range(4):
        span = slice(n * 512, (n + 1) * 512)
        proj[:, span] = jnp.dot(both, w2[:, span], preferred_element_type=F32).astype(BF16)
        copy = pltpu.make_async_copy(proj.at[:, span], out_ref.at[:, span], out_s.at[n])
        copy.start()
        outs.append(copy)
    for copy in outs:
        copy.wait()


def per_device(queries, keys, values, out_weight):
    hbm = pl.BlockSpec(memory_space=pl.ANY)
    dma = pltpu.SemaphoreType.DMA
    return pl.pallas_call(
        attention_kernel,
        out_shape=jax.ShapeDtypeStruct((ROWS, WIDTH), BF16),
        in_specs=[hbm] * 4,
        out_specs=hbm,
        scratch_shapes=[
            pltpu.VMEM((2, LINE, HD), BF16),
            pltpu.VMEM((2, Y * SUPER, HD), BF16),
            pltpu.VMEM((Y, HD, SUPER), BF16),
            pltpu.VMEM((HALF, HD), BF16),
            pltpu.VMEM((2, LINE, 256), F32),
            pltpu.VMEM((2, LINE, 128), F32),
            pltpu.VMEM((2, Z, MESSAGE, HD), BF16),
            pltpu.VMEM((2, Z, MESSAGE, HD), BF16),
            pltpu.VMEM((2, ROWS, HD), BF16),
            pltpu.VMEM((2 * HD, WIDTH), BF16),
            pltpu.VMEM((ROWS, WIDTH), BF16),
            dma((5,)), dma((4,)), dma((4, 4)), dma((16,)), dma, dma((2, 8)), dma((2, 8)), dma((2, 8)), dma((2, 8)),
            dma((2,)), dma((2,)), dma((4,)),
        ],
        compiler_params=pltpu.CompilerParams(
            collective_id=0, has_side_effects=True, vmem_limit_bytes=56 << 20
        ),
    )(queries[0], keys[0], values[0], out_weight[0])


def solution(mesh):
    placed = (
        P("head", "ctx", None),
        P("head", "ctx", None),
        P("head", "ctx", None),
        P("head", None, None),
    )
    return jax.shard_map(
        per_device, mesh=mesh, in_specs=placed, out_specs=P("ctx", "head"), check_vma=False
    )
```

```python
import functools
import math

import jax
import jax.numpy as jnp
from jax import lax
from jax.experimental import pallas as pl
from jax.experimental.pallas import tpu as pltpu
from jax.sharding import PartitionSpec as P

MESH = pl.DeviceIdType.MESH
X, Y, Z = 4, 4, 8
ROWS = 384
HALF = ROWS // 2
HD = 128
LINE = Z * HALF
SUPER = X * ROWS
TILE = LINE // 2
BLOCK = 512
WIDTH = 2048
MESSAGE = HALF + 16
SCALE2 = math.log2(math.e) / math.sqrt(HD)
LOW = -1e30
TINY = 1e-30
BF16, F32 = jnp.bfloat16, jnp.float32


def lane_rows(columns):
    return jnp.concatenate([columns[0:128].T[0:1], columns[HALF - 128 : HALF].T[0:1]], axis=0)


def lane_columns(rows):
    low = jnp.broadcast_to(rows[0:1], (128, 128)).T
    high = jnp.broadcast_to(rows[1:2], (128, 128)).T
    return jnp.concatenate([low, high[256 - HALF : 128]], axis=0)


def pack_stats(rows):
    high = rows.astype(BF16).astype(F32)
    mid = (rows - high).astype(BF16).astype(F32)
    low = rows - high - mid
    return jnp.concatenate([high, mid, low, jnp.zeros((10, 128), F32)], axis=0).astype(BF16)


def unpack_stats(packed):
    wide = packed.astype(F32)
    return wide[0:2] + wide[2:4] + wide[4:6]


def attention_kernel(
    q_ref, k_ref, v_ref, w_ref, out_ref,
    qbuf, kvbuf, kt, swap, acc, top, obuf, rbuf, att, w2, proj,
    in_s, kv1_ss, kv2_ss, kv_rs, swap_ss, q_ss, q_rs, o_ss, o_rs, c_ss, c_rs, out_s,
):
    index, core = lax.axis_index("ctx"), lax.axis_index("head")
    x, z, y = lax.rem(index, X), lax.rem(lax.div(index, X), Z), lax.div(index, X * Z)
    ym = Y - 1 - y
    near = lax.div(z, 4)

    def at(px, py, pz, pc=None):
        return ((py * Z + pz) * X + px, core if pc is None else pc)

    def ring(p, d, n):
        return lax.rem(p + d + n, n)

    def remote(src, dst, ss, rs, where):
        return pltpu.make_async_remote_copy(
            src_ref=src, dst_ref=dst, send_sem=ss, recv_sem=rs, device_id=where, device_id_type=MESH
        )

    other = 1 - core
    partner = at(x, y, z, other)
    x_peers = [at(ring(x, k, X), y, z) for k in range(1, X)]
    y_peers = [at(x, ring(y, k, Y), z) for k in range(1, Y)]
    lines = [[at(x, yy, ring(z, k, Z)) for k in range(Z)] for yy in (y, ym)]
    first = [(jnp.where(core == 0, a[0], b[0]), core) for a, b in zip(x_peers, y_peers)]
    second = [(jnp.where(core == 0, b[0], a[0]), core) for a, b in zip(x_peers, y_peers)]

    def rows_at(n, size):
        return pl.ds(pl.multiple_of(n * size, size), size)

    def chunk(n):
        return kvbuf.at[:, rows_at(n, ROWS), :]

    mine = y * X + x
    loads = [
        pltpu.make_async_copy(k_ref, kvbuf.at[0, rows_at(mine, ROWS)], in_s.at[0]),
        pltpu.make_async_copy(v_ref, kvbuf.at[1, rows_at(mine, ROWS)], in_s.at[1]),
        pltpu.make_async_copy(q_ref.at[0:HALF], qbuf.at[0, rows_at(z, HALF)], in_s.at[2]),
        pltpu.make_async_copy(q_ref.at[HALF:ROWS], swap, in_s.at[3]),
        pltpu.make_async_copy(
            w_ref.at[:, rows_at(core, WIDTH)], w2.at[rows_at(core, HD)], in_s.at[4]
        ),
    ]
    for copy in loads:
        copy.start()

    barrier = pltpu.get_barrier_semaphore()
    for where in lines[0][1:] + lines[1] + x_peers + y_peers + [partner]:
        pl.semaphore_signal(barrier, inc=1, device_id=where, device_id_type=MESH)
    pl.semaphore_wait(barrier, 22)

    sent = []

    def when(condition, act):
        if condition is None:
            act()
        else:
            pl.when(condition)(act)

    def send(copy, condition=None):
        when(condition, copy.start)
        sent.append((condition, copy))

    def needed(source, target):
        return (source <= target) | (source <= Y - 1 - target)

    y_targets = [needed(y, ring(y, k, Y)) for k in range(1, Y)]

    for copy in loads[:4]:
        copy.wait()
    for k in (1, 3, 2):
        used = (core == 0) | y_targets[k - 1]
        send(remote(chunk(mine), chunk(mine), kv1_ss.at[k], kv_rs.at[mine], first[k - 1]), used)
    own_rows = [qbuf.at[h, rows_at(z, HALF)] for h in range(2)]
    send(remote(swap, own_rows[1], swap_ss, q_rs.at[1, z], lines[1][0]))
    for k in (1, 7, 2, 6, 3, 5, 4):
        send(remote(own_rows[0], own_rows[0], q_ss.at[0, k], q_rs.at[0, z], lines[0][k]))
    for k in (1, 3, 2):
        used = (core == 1) | y_targets[k - 1]
        send(remote(chunk(mine), chunk(mine), kv2_ss.at[0, k], kv_rs.at[mine], second[k - 1]), used)
    remote(own_rows[1], own_rows[1], swap_ss, q_rs.at[1, z], partner).wait_recv()
    for k in (1, 7, 2, 6, 3, 5, 4):
        send(remote(own_rows[1], own_rows[1], q_ss.at[1, k], q_rs.at[1, z], lines[0][k]))
    send(
        remote(
            w_ref.at[:, rows_at(other, WIDTH)], w2.at[rows_at(core, HD)], c_ss.at[0], c_rs.at[0], partner
        )
    )

    def clear(n, _):
        acc[n] = jnp.zeros((LINE, 256), F32)
        top[n] = jnp.full((LINE, 128), LOW, F32)
        return 0

    lax.fori_loop(0, 2, clear, 0)

    for j, k in enumerate((1, 3, 2)):
        source = jnp.where(jnp.int32(j) >= y, j + 1, j)
        n = jnp.where(core == 0, y * X + ring(x, -k, X), source * X + x)
        came = (core == 0) | needed(source, y)
        when(came, remote(chunk(n), chunk(n), kv1_ss.at[j], kv_rs.at[n], partner).wait_recv)
        for k in (1, 3, 2):
            used = jnp.where(core == 0, y_targets[k - 1], came)
            send(remote(chunk(n), chunk(n), kv2_ss.at[j + 1, k], kv_rs.at[n], second[k - 1]), used)

    def spread(parts):
        highest = jnp.max(functools.reduce(jnp.maximum, parts), axis=1, keepdims=True)
        return jnp.broadcast_to(highest, parts[0].shape)

    def twice(a):
        return jnp.concatenate([a, a], axis=1)

    def weigh(pieces, new):
        return jnp.concatenate([jnp.exp2((one - new) * SCALE2).astype(BF16) for one in pieces], axis=1)

    def score(h, span, yp, b):
        keys = kt[yp, :, b * BLOCK : (b + 1) * BLOCK]
        both = jnp.dot(qbuf[h, span, :], keys, preferred_element_type=F32)
        return [both[:, n * 128 : (n + 1) * 128] for n in range(BLOCK // 128)]

    def values_of(yp, start, count):
        values = kvbuf[1, pl.ds(pl.multiple_of(yp * SUPER + start, BLOCK), count), :]
        return jnp.concatenate([values, jnp.ones(values.shape, BF16)], axis=1)

    def attend(h, g, yp):
        spans = [pl.ds(pl.multiple_of(g * TILE + t * ROWS, ROWS), ROWS) for t in range(TILE // ROWS)]

        def scores(span):
            return [piece for b in range(SUPER // BLOCK) for piece in score(h, span, yp, b)]

        pieces = scores(spans[0])
        for t, span in enumerate(spans):
            later = scores(spans[t + 1]) if t + 1 < len(spans) else None
            old = top[h, span, :]
            new = jnp.maximum(old, spread(pieces))
            added = jnp.dot(weigh(pieces, new), values_of(yp, 0, SUPER), preferred_element_type=F32)
            acc[h, span, :] = acc[h, span, :] * twice(jnp.exp2((old - new) * SCALE2)) + added
            top[h, span, :] = new
            pieces = later

    def attend_below(h, i, yp, limit):
        span = pl.ds(pl.multiple_of(i * ROWS, ROWS), ROWS)
        lane = lax.broadcasted_iota(jnp.int32, (ROWS, 128), 1)

        def kept(b):
            pieces = score(h, span, yp, b)
            return [
                jnp.where(lane + (b * BLOCK + n * 128) <= limit, one, LOW) for n, one in enumerate(pieces)
            ]

        old, summed = top[h, span, :], acc[h, span, :]
        pieces = kept(0)
        for b in range(SUPER // BLOCK):
            later = kept(b + 1) if b + 1 < SUPER // BLOCK else None
            new = jnp.maximum(old, spread(pieces))
            added = jnp.dot(
                weigh(pieces, new), values_of(yp, b * BLOCK, BLOCK), preferred_element_type=F32
            )
            summed = summed * twice(jnp.exp2((old - new) * SCALE2)) + added
            old, pieces = new, later
        top[h, span, :] = old
        acc[h, span, :] = summed

    def task(h, g, yp):
        yq = jnp.where(h == 0, y, ym)

        @pl.when((yp < yq) | ((yp == yq) & (g > near)))
        def _():
            attend(h, g, yp)

        @pl.when((yp == yq) & (g == near))
        def _():
            edge = lax.div(z, 2)

            def pair(i, _):
                row = lax.broadcasted_iota(jnp.int32, (ROWS, 128), 0)
                here = row + (x * ROWS + h * HALF)
                even = lax.rem(z, 2) == 0
                low = jnp.where(even, here, -1)
                high = jnp.where(even, SUPER, here - HALF)
                limit = jnp.where(row < HALF, low, high)
                attend_below(h, i, yp, jnp.where(i > edge, SUPER, limit))
                return 0

            lax.fori_loop(edge, 2 * g + 2, pair, 0)

    def need_keys(yp):
        for xp in range(X):
            n = yp * X + xp

            @pl.when(jnp.where(core == 0, yp != y, x != xp))
            def _():
                remote(chunk(n), chunk(n), kv1_ss.at[0], kv_rs.at[n], partner).wait_recv()

        for p in range(4):
            rows = pl.ds(pl.multiple_of(yp * SUPER + ROWS * p, ROWS), ROWS)
            kt[yp, :, ROWS * p : ROWS * (p + 1)] = kvbuf[0, rows, :].T

    def need_queries(h, g):
        for t in range(4):
            s = 4 * g + t

            @pl.when(s != z)
            def _():
                r = qbuf.at[h, rows_at(s, HALF)]
                remote(r, r, q_ss.at[0, 0], q_rs.at[h, s], partner).wait_recv()

    def o_copy(h, s):
        where = at(x, jnp.where(h == 0, y, ym), s)
        return remote(obuf.at[h, s], rbuf.at[h, z], o_ss.at[h, s], o_rs.at[h, z], where)

    def finish(h, g):
        def one(t, _):
            s = 4 * g + t
            span = rows_at(s, HALF)
            total = jnp.maximum(acc[h, span, 128:256], TINY)
            obuf[h, s, 0:HALF, :] = (acc[h, span, 0:128] / total).astype(BF16)
            stats = top[h, span, :] * SCALE2 + jnp.log2(total)
            obuf[h, s, HALF:MESSAGE, :] = pack_stats(lane_rows(stats))

            @pl.when((h == 1) | (s != z))
            def _():
                o_copy(h, s).start()

            @pl.when((h == 0) & (s == z))
            def _():
                rbuf[0, z] = obuf[0, z]

            return 0

        lax.fori_loop(0, 4, one, 0)

    last = [jnp.maximum(y - 1, 0), ym]

    def superblock(e, _):
        yp = jnp.where(e == 0, y, jnp.where(e - 1 >= y, e, e - 1))
        need_keys(yp)

        def group(i, _):
            h = jnp.where(lax.div(i, 2) == 0, jnp.where(y < ym, 0, 1), jnp.where(y < ym, 1, 0))
            g = jnp.where(lax.rem(i, 2) == 0, 1 - near, near)

            @pl.when(e == 0)
            def _():
                need_queries(h, g)

            task(h, g, yp)

            @pl.when(yp == jnp.where(h == 0, last[0], last[1]))
            def _():
                finish(h, g)

            return 0

        lax.fori_loop(0, 4, group, 0)
        return 0

    lax.fori_loop(0, jnp.maximum(y, ym) + 1, superblock, 0)

    def merge(h, _):
        for s in range(Z):

            @pl.when((h == 1) | (z != s))
            def _():
                remote(rbuf.at[h, s], rbuf.at[h, s], o_ss.at[0, 0], o_rs.at[h, s], partner).wait_recv()

        stats = [unpack_stats(rbuf[h, s, HALF:MESSAGE, :]) for s in range(Z)]
        highest = functools.reduce(jnp.maximum, stats)
        shares = [jnp.exp2(one - highest) for one in stats]
        total = functools.reduce(jnp.add, shares)
        merged = jnp.zeros((HALF, HD), F32)
        for s in range(Z):
            merged = merged + rbuf[h, s, 0:HALF, :].astype(F32) * lane_columns(shares[s] / total)
        att[core, rows_at(h, HALF), :] = merged.astype(BF16)
        return 0

    lax.fori_loop(0, 2, merge, 0)
    att_copy = remote(att.at[core], att.at[core], c_ss.at[1], c_rs.at[1], partner)
    att_copy.start()

    for condition, copy in sent:
        when(condition, copy.wait_send)

    def drain(s, _):
        for h in range(2):

            @pl.when((h == 1) | (s != z))
            def _():
                o_copy(h, s).wait_send()

        return 0

    lax.fori_loop(0, Z, drain, 0)
    loads[4].wait()
    w_other = w2.at[rows_at(other, HD)]
    remote(w_other, w_other, c_ss.at[0], c_rs.at[0], partner).wait_recv()
    att_copy.wait_send()
    remote(att.at[other], att.at[other], c_ss.at[1], c_rs.at[1], partner).wait_recv()
    both = jnp.concatenate([att[0], att[1]], axis=1)
    for n in range(4):
        span = slice(n * 512, (n + 1) * 512)
        out_ref[:, span] = jnp.dot(both, w2[:, span], preferred_element_type=F32).astype(BF16)


def per_device(queries, keys, values, out_weight):
    hbm = pl.BlockSpec(memory_space=pl.ANY)
    dma = pltpu.SemaphoreType.DMA
    return pl.pallas_call(
        attention_kernel,
        out_shape=pltpu.VMEM((ROWS, WIDTH), BF16),
        in_specs=[hbm] * 4,
        out_specs=pl.BlockSpec(memory_space=pltpu.VMEM),
        scratch_shapes=[
            pltpu.VMEM((2, LINE, HD), BF16),
            pltpu.VMEM((2, Y * SUPER, HD), BF16),
            pltpu.VMEM((Y, HD, SUPER), BF16),
            pltpu.VMEM((HALF, HD), BF16),
            pltpu.VMEM((2, LINE, 256), F32),
            pltpu.VMEM((2, LINE, 128), F32),
            pltpu.VMEM((2, Z, MESSAGE, HD), BF16),
            pltpu.VMEM((2, Z, MESSAGE, HD), BF16),
            pltpu.VMEM((2, ROWS, HD), BF16),
            pltpu.VMEM((2 * HD, WIDTH), BF16),
            pltpu.VMEM((ROWS, WIDTH), BF16),
            dma((5,)), dma((4,)), dma((4, 4)), dma((16,)), dma, dma((2, 8)), dma((2, 8)), dma((2, 8)), dma((2, 8)),
            dma((2,)), dma((2,)), dma((4,)),
        ],
        compiler_params=pltpu.CompilerParams(
            collective_id=0, has_side_effects=True, vmem_limit_bytes=56 << 20
        ),
    )(queries[0], keys[0], values[0], out_weight[0])


def solution(mesh):
    placed = (
        P("head", "ctx", None),
        P("head", "ctx", None),
        P("head", "ctx", None),
        P("head", None, None),
    )
    return jax.shard_map(
        per_device, mesh=mesh, in_specs=placed, out_specs=P("ctx", "head"), check_vma=False
    )
```

```python
import functools
import math

import jax
import jax.numpy as jnp
from jax import lax
from jax.experimental import pallas as pl
from jax.experimental.pallas import tpu as pltpu
from jax.sharding import PartitionSpec as P

MESH = pl.DeviceIdType.MESH
X, Y, Z = 4, 4, 8
ROWS = 384
HALF = ROWS // 2
HD = 128
LINE = Z * HALF
SUPER = X * ROWS
TILE = LINE // 2
BLOCK = 512
WIDTH = 2048
MESSAGE = HALF + 16
SCALE2 = math.log2(math.e) / math.sqrt(HD)
LOW = -1e30
TINY = 1e-30
BF16, F32 = jnp.bfloat16, jnp.float32


def lane_rows(columns):
    return jnp.concatenate([columns[0:128].T[0:1], columns[HALF - 128 : HALF].T[0:1]], axis=0)


def lane_columns(rows):
    low = jnp.broadcast_to(rows[0:1], (128, 128)).T
    high = jnp.broadcast_to(rows[1:2], (128, 128)).T
    return jnp.concatenate([low, high[256 - HALF : 128]], axis=0)


def pack_stats(rows):
    high = rows.astype(BF16).astype(F32)
    mid = (rows - high).astype(BF16).astype(F32)
    low = rows - high - mid
    return jnp.concatenate([high, mid, low, jnp.zeros((10, 128), F32)], axis=0).astype(BF16)


def unpack_stats(packed):
    wide = packed.astype(F32)
    return wide[0:2] + wide[2:4] + wide[4:6]


def attention_kernel(
    q_ref, k_ref, v_ref, w_ref, out_ref,
    qbuf, kvbuf, kt, swap, acc, top, obuf, rbuf, att, w2,
    in_s, kv1_ss, kv2_ss, kv_rs, swap_ss, q_ss, q_rs, o_ss, o_rs, c_ss, c_rs,
):
    index, core = lax.axis_index("ctx"), lax.axis_index("head")
    x, z, y = lax.rem(index, X), lax.rem(lax.div(index, X), Z), lax.div(index, X * Z)
    ym = Y - 1 - y
    near = lax.div(z, 4)

    def at(px, py, pz, pc=None):
        return ((py * Z + pz) * X + px, core if pc is None else pc)

    def ring(p, d, n):
        return lax.rem(p + d + n, n)

    def remote(src, dst, ss, rs, where):
        return pltpu.make_async_remote_copy(
            src_ref=src, dst_ref=dst, send_sem=ss, recv_sem=rs, device_id=where, device_id_type=MESH
        )

    other = 1 - core
    partner = at(x, y, z, other)
    x_peers = [at(ring(x, k, X), y, z) for k in range(1, X)]
    y_peers = [at(x, ring(y, k, Y), z) for k in range(1, Y)]
    lines = [[at(x, yy, ring(z, k, Z)) for k in range(Z)] for yy in (y, ym)]
    first = [(jnp.where(core == 0, a[0], b[0]), core) for a, b in zip(x_peers, y_peers)]
    second = [(jnp.where(core == 0, b[0], a[0]), core) for a, b in zip(x_peers, y_peers)]

    def rows_at(n, size):
        return pl.ds(pl.multiple_of(n * size, size), size)

    def chunk(n):
        return kvbuf.at[:, rows_at(n, ROWS), :]

    mine = y * X + x
    loads = [
        pltpu.make_async_copy(k_ref, kvbuf.at[0, rows_at(mine, ROWS)], in_s.at[0]),
        pltpu.make_async_copy(v_ref, kvbuf.at[1, rows_at(mine, ROWS)], in_s.at[1]),
        pltpu.make_async_copy(q_ref.at[0:HALF], qbuf.at[0, rows_at(z, HALF)], in_s.at[2]),
        pltpu.make_async_copy(q_ref.at[HALF:ROWS], swap, in_s.at[3]),
        pltpu.make_async_copy(
            w_ref.at[:, rows_at(core, WIDTH)], w2.at[rows_at(core, HD)], in_s.at[4]
        ),
    ]
    for copy in loads:
        copy.start()

    barrier = pltpu.get_barrier_semaphore()
    for where in lines[0][1:] + lines[1] + x_peers + y_peers + [partner]:
        pl.semaphore_signal(barrier, inc=1, device_id=where, device_id_type=MESH)
    pl.semaphore_wait(barrier, 22)

    sent = []

    def when(condition, act):
        if condition is None:
            act()
        else:
            pl.when(condition)(act)

    def send(copy, condition=None):
        when(condition, copy.start)
        sent.append((condition, copy))

    def needed(source, target):
        return (source <= target) | (source <= Y - 1 - target)

    y_targets = [needed(y, ring(y, k, Y)) for k in range(1, Y)]

    for copy in loads[:4]:
        copy.wait()
    for k in (1, 3, 2):
        used = (core == 0) | y_targets[k - 1]
        send(remote(chunk(mine), chunk(mine), kv1_ss.at[k], kv_rs.at[mine], first[k - 1]), used)
    own_rows = [qbuf.at[h, rows_at(z, HALF)] for h in range(2)]
    send(remote(swap, own_rows[1], swap_ss, q_rs.at[1, z], lines[1][0]))
    for k in (1, 7, 2, 6, 3, 5, 4):
        send(remote(own_rows[0], own_rows[0], q_ss.at[0, k], q_rs.at[0, z], lines[0][k]))
    for k in (1, 3, 2):
        used = (core == 1) | y_targets[k - 1]
        send(remote(chunk(mine), chunk(mine), kv2_ss.at[0, k], kv_rs.at[mine], second[k - 1]), used)
    remote(own_rows[1], own_rows[1], swap_ss, q_rs.at[1, z], partner).wait_recv()
    for k in (1, 7, 2, 6, 3, 5, 4):
        send(remote(own_rows[1], own_rows[1], q_ss.at[1, k], q_rs.at[1, z], lines[0][k]))
    send(
        remote(
            w_ref.at[:, rows_at(other, WIDTH)], w2.at[rows_at(core, HD)], c_ss.at[0], c_rs.at[0], partner
        )
    )

    def clear(n, _):
        acc[n] = jnp.zeros((LINE, 256), F32)
        top[n] = jnp.full((LINE, 128), LOW, F32)
        return 0

    lax.fori_loop(0, 2, clear, 0)

    for j, k in enumerate((1, 3, 2)):
        source = jnp.where(jnp.int32(j) >= y, j + 1, j)
        n = jnp.where(core == 0, y * X + ring(x, -k, X), source * X + x)
        came = (core == 0) | needed(source, y)
        when(came, remote(chunk(n), chunk(n), kv1_ss.at[j], kv_rs.at[n], partner).wait_recv)
        for k in (1, 3, 2):
            used = jnp.where(core == 0, y_targets[k - 1], came)
            send(remote(chunk(n), chunk(n), kv2_ss.at[j + 1, k], kv_rs.at[n], second[k - 1]), used)

    def spread(parts):
        highest = jnp.max(functools.reduce(jnp.maximum, parts), axis=1, keepdims=True)
        return jnp.broadcast_to(highest, parts[0].shape)

    def twice(a):
        return jnp.concatenate([a, a], axis=1)

    def weigh(pieces, new):
        return jnp.concatenate([jnp.exp2((one - new) * SCALE2).astype(BF16) for one in pieces], axis=1)

    def score(h, span, yp, b):
        keys = kt[yp, :, b * BLOCK : (b + 1) * BLOCK]
        both = jnp.dot(qbuf[h, span, :], keys, preferred_element_type=F32)
        return [both[:, n * 128 : (n + 1) * 128] for n in range(BLOCK // 128)]

    def values_of(yp, start, count):
        values = kvbuf[1, pl.ds(pl.multiple_of(yp * SUPER + start, BLOCK), count), :]
        return jnp.concatenate([values, jnp.ones(values.shape, BF16)], axis=1)

    def attend(h, g, yp):
        spans = [pl.ds(pl.multiple_of(g * TILE + t * ROWS, ROWS), ROWS) for t in range(TILE // ROWS)]

        def scores(span):
            return [piece for b in range(SUPER // BLOCK) for piece in score(h, span, yp, b)]

        pieces = scores(spans[0])
        for t, span in enumerate(spans):
            later = scores(spans[t + 1]) if t + 1 < len(spans) else None
            old = top[h, span, :]
            new = jnp.maximum(old, spread(pieces))
            added = jnp.dot(weigh(pieces, new), values_of(yp, 0, SUPER), preferred_element_type=F32)
            acc[h, span, :] = acc[h, span, :] * twice(jnp.exp2((old - new) * SCALE2)) + added
            top[h, span, :] = new
            pieces = later

    def attend_below(h, i, yp, limit):
        span = pl.ds(pl.multiple_of(i * ROWS, ROWS), ROWS)
        lane = lax.broadcasted_iota(jnp.int32, (ROWS, 128), 1)

        def kept(b):
            pieces = score(h, span, yp, b)
            return [
                jnp.where(lane + (b * BLOCK + n * 128) <= limit, one, LOW) for n, one in enumerate(pieces)
            ]

        old, summed = top[h, span, :], acc[h, span, :]
        pieces = kept(0)
        for b in range(SUPER // BLOCK):
            later = kept(b + 1) if b + 1 < SUPER // BLOCK else None
            new = jnp.maximum(old, spread(pieces))
            added = jnp.dot(
                weigh(pieces, new), values_of(yp, b * BLOCK, BLOCK), preferred_element_type=F32
            )
            summed = summed * twice(jnp.exp2((old - new) * SCALE2)) + added
            old, pieces = new, later
        top[h, span, :] = old
        acc[h, span, :] = summed

    def task(h, g, yp):
        yq = jnp.where(h == 0, y, ym)

        @pl.when((yp < yq) | ((yp == yq) & (g > near)))
        def _():
            attend(h, g, yp)

        @pl.when((yp == yq) & (g == near))
        def _():
            edge = lax.div(z, 2)

            def pair(i, _):
                row = lax.broadcasted_iota(jnp.int32, (ROWS, 128), 0)
                here = row + (x * ROWS + h * HALF)
                even = lax.rem(z, 2) == 0
                low = jnp.where(even, here, -1)
                high = jnp.where(even, SUPER, here - HALF)
                limit = jnp.where(row < HALF, low, high)
                attend_below(h, i, yp, jnp.where(i > edge, SUPER, limit))
                return 0

            lax.fori_loop(edge, 2 * g + 2, pair, 0)

    def need_keys(yp):
        for xp in range(X):
            n = yp * X + xp

            @pl.when(jnp.where(core == 0, yp != y, x != xp))
            def _():
                remote(chunk(n), chunk(n), kv1_ss.at[0], kv_rs.at[n], partner).wait_recv()

        for p in range(4):
            rows = pl.ds(pl.multiple_of(yp * SUPER + ROWS * p, ROWS), ROWS)
            kt[yp, :, ROWS * p : ROWS * (p + 1)] = kvbuf[0, rows, :].T

    def need_queries(h, g):
        for t in range(4):
            s = 4 * g + t

            @pl.when(s != z)
            def _():
                r = qbuf.at[h, rows_at(s, HALF)]
                remote(r, r, q_ss.at[0, 0], q_rs.at[h, s], partner).wait_recv()

    def o_copy(h, s):
        where = at(x, jnp.where(h == 0, y, ym), s)
        return remote(obuf.at[h, s], rbuf.at[h, z], o_ss.at[h, s], o_rs.at[h, z], where)

    def finish(h, g):
        def one(t, _):
            s = 4 * g + t
            span = rows_at(s, HALF)
            total = jnp.maximum(acc[h, span, 128:256], TINY)
            obuf[h, s, 0:HALF, :] = (acc[h, span, 0:128] / total).astype(BF16)
            stats = top[h, span, :] * SCALE2 + jnp.log2(total)
            obuf[h, s, HALF:MESSAGE, :] = pack_stats(lane_rows(stats))

            @pl.when((h == 1) | (s != z))
            def _():
                o_copy(h, s).start()

            @pl.when((h == 0) & (s == z))
            def _():
                rbuf[0, z] = obuf[0, z]

            return 0

        lax.fori_loop(0, 4, one, 0)

    count = jnp.maximum(y, ym) + 1

    def superblock(e):
        return jnp.where(e == 0, y, jnp.where(e - 1 >= y, e, e - 1))

    def need_more(e, _):
        need_keys(superblock(e))
        return 0

    def work(i, _):
        early = i < 4
        n = jnp.where(early, i, i - 4)
        before = jnp.where(y < ym, 0, 1)
        h = jnp.where(early, lax.rem(n, 2), jnp.where(lax.div(n, 2) == 0, before, 1 - before))
        close = jnp.where(early, lax.div(n, 2) == 0, lax.rem(n, 2) == 1)
        g = jnp.where(close, near, 1 - near)

        @pl.when(i == 0)
        def _():
            need_keys(y)

        @pl.when(early)
        def _():
            need_queries(h, g)

        @pl.when(i == 4)
        def _():
            lax.fori_loop(1, count, need_more, 0)

        def one(e, _):
            task(h, g, superblock(e))
            return 0

        lax.fori_loop(jnp.where(early, 0, 1), jnp.where(early, 1, count), one, 0)

        @pl.when(early == ((y == 0) & (h == 0)))
        def _():
            finish(h, g)

        return 0

    lax.fori_loop(0, 8, work, 0)

    def merge(h, _):
        for s in range(Z):

            @pl.when((h == 1) | (z != s))
            def _():
                remote(rbuf.at[h, s], rbuf.at[h, s], o_ss.at[0, 0], o_rs.at[h, s], partner).wait_recv()

        stats = [unpack_stats(rbuf[h, s, HALF:MESSAGE, :]) for s in range(Z)]
        highest = functools.reduce(jnp.maximum, stats)
        shares = [jnp.exp2(one - highest) for one in stats]
        total = functools.reduce(jnp.add, shares)
        merged = jnp.zeros((HALF, HD), F32)
        for s in range(Z):
            merged = merged + rbuf[h, s, 0:HALF, :].astype(F32) * lane_columns(shares[s] / total)
        att[core, rows_at(h, HALF), :] = merged.astype(BF16)
        att_copy(h, core).start()
        return 0

    def att_copy(h, c):
        rows = att.at[c, rows_at(h, HALF)]
        return remote(rows, rows, c_ss.at[1 + h], c_rs.at[1 + h], partner)

    lax.fori_loop(0, 2, merge, 0)

    for condition, copy in sent:
        when(condition, copy.wait_send)

    def drain(s, _):
        for h in range(2):

            @pl.when((h == 1) | (s != z))
            def _():
                o_copy(h, s).wait_send()

        return 0

    lax.fori_loop(0, Z, drain, 0)
    loads[4].wait()
    w_other = w2.at[rows_at(other, HD)]
    remote(w_other, w_other, c_ss.at[0], c_rs.at[0], partner).wait_recv()
    for h in range(2):
        span = slice(h * HALF, (h + 1) * HALF)
        att_copy(h, other).wait_recv()
        both = jnp.concatenate([att[0, span, :], att[1, span, :]], axis=1)
        for n in range(4):
            columns = slice(n * 512, (n + 1) * 512)
            out_ref[span, columns] = jnp.dot(both, w2[:, columns], preferred_element_type=F32).astype(BF16)
    for h in range(2):
        att_copy(h, core).wait_send()


def per_device(queries, keys, values, out_weight):
    hbm = pl.BlockSpec(memory_space=pl.ANY)
    dma = pltpu.SemaphoreType.DMA
    return pl.pallas_call(
        attention_kernel,
        out_shape=pltpu.VMEM((ROWS, WIDTH), BF16),
        in_specs=[hbm] * 4,
        out_specs=pl.BlockSpec(memory_space=pltpu.VMEM),
        scratch_shapes=[
            pltpu.VMEM((2, LINE, HD), BF16),
            pltpu.VMEM((2, Y * SUPER, HD), BF16),
            pltpu.VMEM((Y, HD, SUPER), BF16),
            pltpu.VMEM((HALF, HD), BF16),
            pltpu.VMEM((2, LINE, 256), F32),
            pltpu.VMEM((2, LINE, 128), F32),
            pltpu.VMEM((2, Z, MESSAGE, HD), BF16),
            pltpu.VMEM((2, Z, MESSAGE, HD), BF16),
            pltpu.VMEM((2, ROWS, HD), BF16),
            pltpu.VMEM((2 * HD, WIDTH), BF16),
            dma((5,)), dma((4,)), dma((4, 4)), dma((16,)), dma, dma((2, 8)), dma((2, 8)), dma((2, 8)), dma((2, 8)),
            dma((3,)), dma((3,)),
        ],
        compiler_params=pltpu.CompilerParams(
            collective_id=0, has_side_effects=True, vmem_limit_bytes=56 << 20
        ),
    )(queries[0], keys[0], values[0], out_weight[0])


def solution(mesh):
    placed = (
        P("head", "ctx", None),
        P("head", "ctx", None),
        P("head", "ctx", None),
        P("head", None, None),
    )
    return jax.shard_map(
        per_device, mesh=mesh, in_specs=placed, out_specs=P("ctx", "head"), check_vma=False
    )
```

```python
import functools
import math

import jax
import jax.numpy as jnp
from jax import lax
from jax.experimental import pallas as pl
from jax.experimental.pallas import tpu as pltpu
from jax.sharding import PartitionSpec as P

MESH = pl.DeviceIdType.MESH
X, Y, Z = 4, 4, 8
ROWS = 384
HALF = ROWS // 2
HD = 128
LINE = Z * HALF
SUPER = X * ROWS
TILE = LINE // 2
BLOCK = 512
WIDTH = 2048
MESSAGE = HALF + 16
SCALE2 = math.log2(math.e) / math.sqrt(HD)
LOW = -1e30
TINY = 1e-30
BF16, F32 = jnp.bfloat16, jnp.float32


def lane_rows(columns):
    return jnp.concatenate([columns[0:128].T[0:1], columns[HALF - 128 : HALF].T[0:1]], axis=0)


def lane_columns(rows):
    low = jnp.broadcast_to(rows[0:1], (128, 128)).T
    high = jnp.broadcast_to(rows[1:2], (128, 128)).T
    return jnp.concatenate([low, high[256 - HALF : 128]], axis=0)


def pack_stats(rows):
    high = rows.astype(BF16).astype(F32)
    mid = (rows - high).astype(BF16).astype(F32)
    low = rows - high - mid
    return jnp.concatenate([high, mid, low, jnp.zeros((10, 128), F32)], axis=0).astype(BF16)


def unpack_stats(packed):
    wide = packed.astype(F32)
    return wide[0:2] + wide[2:4] + wide[4:6]


def attention_kernel(
    q_ref, k_ref, v_ref, w_ref, out_ref,
    qbuf, kvbuf, kt, swap, acc, top, obuf, rbuf, att, w2,
    in_s, kv1_ss, kv2_ss, kv_rs, swap_ss, q_ss, q_rs, o_ss, o_rs, c_ss, c_rs,
):
    index, core = lax.axis_index("ctx"), lax.axis_index("head")
    x, z, y = lax.rem(index, X), lax.rem(lax.div(index, X), Z), lax.div(index, X * Z)
    ym = Y - 1 - y
    near = lax.div(z, 4)

    def at(px, py, pz, pc=None):
        return ((py * Z + pz) * X + px, core if pc is None else pc)

    def ring(p, d, n):
        return lax.rem(p + d + n, n)

    def remote(src, dst, ss, rs, where):
        return pltpu.make_async_remote_copy(
            src_ref=src, dst_ref=dst, send_sem=ss, recv_sem=rs, device_id=where, device_id_type=MESH
        )

    other = 1 - core
    partner = at(x, y, z, other)
    x_peers = [at(ring(x, k, X), y, z) for k in range(1, X)]
    y_peers = [at(x, ring(y, k, Y), z) for k in range(1, Y)]
    lines = [[at(x, yy, ring(z, k, Z)) for k in range(Z)] for yy in (y, ym)]
    first = [(jnp.where(core == 0, a[0], b[0]), core) for a, b in zip(x_peers, y_peers)]
    second = [(jnp.where(core == 0, b[0], a[0]), core) for a, b in zip(x_peers, y_peers)]

    def rows_at(n, size):
        return pl.ds(pl.multiple_of(n * size, size), size)

    def chunk(n):
        return kvbuf.at[:, rows_at(n, ROWS), :]

    mine = y * X + x
    loads = [
        pltpu.make_async_copy(k_ref, kvbuf.at[0, rows_at(mine, ROWS)], in_s.at[0]),
        pltpu.make_async_copy(v_ref, kvbuf.at[1, rows_at(mine, ROWS)], in_s.at[1]),
        pltpu.make_async_copy(q_ref.at[0:HALF], qbuf.at[0, rows_at(z, HALF)], in_s.at[2]),
        pltpu.make_async_copy(q_ref.at[HALF:ROWS], swap, in_s.at[3]),
        pltpu.make_async_copy(
            w_ref.at[:, rows_at(core, WIDTH)], w2.at[rows_at(core, HD)], in_s.at[4]
        ),
    ]
    for copy in loads:
        copy.start()

    barrier = pltpu.get_barrier_semaphore()
    for where in lines[0][1:] + lines[1] + x_peers + y_peers + [partner]:
        pl.semaphore_signal(barrier, inc=1, device_id=where, device_id_type=MESH)
    pl.semaphore_wait(barrier, 22)

    sent = []

    def when(condition, act):
        if condition is None:
            act()
        else:
            pl.when(condition)(act)

    def send(copy, condition=None):
        when(condition, copy.start)
        sent.append((condition, copy))

    def needed(source, target):
        return (source <= target) | (source <= Y - 1 - target)

    y_targets = [needed(y, ring(y, k, Y)) for k in range(1, Y)]

    for copy in loads[:4]:
        copy.wait()
    for k in (1, 3, 2):
        used = (core == 0) | y_targets[k - 1]
        send(remote(chunk(mine), chunk(mine), kv1_ss.at[k], kv_rs.at[mine], first[k - 1]), used)
    own_rows = [qbuf.at[h, rows_at(z, HALF)] for h in range(2)]
    send(remote(swap, own_rows[1], swap_ss, q_rs.at[1, z], lines[1][0]))
    for k in (1, 7, 2, 6, 3, 5, 4):
        send(remote(own_rows[0], own_rows[0], q_ss.at[0, k], q_rs.at[0, z], lines[0][k]))
    remote(own_rows[1], own_rows[1], swap_ss, q_rs.at[1, z], partner).wait_recv()
    for k in (1, 7, 2, 6, 3, 5, 4):
        send(remote(own_rows[1], own_rows[1], q_ss.at[1, k], q_rs.at[1, z], lines[0][k]))
    for k in (1, 3, 2):
        used = (core == 1) | y_targets[k - 1]
        send(remote(chunk(mine), chunk(mine), kv2_ss.at[0, k], kv_rs.at[mine], second[k - 1]), used)
    send(
        remote(
            w_ref.at[:, rows_at(other, WIDTH)], w2.at[rows_at(core, HD)], c_ss.at[0], c_rs.at[0], partner
        )
    )

    def clear(n, _):
        acc[n] = jnp.zeros((LINE, 256), F32)
        top[n] = jnp.full((LINE, 128), LOW, F32)
        return 0

    lax.fori_loop(0, 2, clear, 0)

    for j, k in enumerate((1, 3, 2)):
        source = jnp.where(jnp.int32(j) >= y, j + 1, j)
        n = jnp.where(core == 0, y * X + ring(x, -k, X), source * X + x)
        came = (core == 0) | needed(source, y)
        when(came, remote(chunk(n), chunk(n), kv1_ss.at[j], kv_rs.at[n], partner).wait_recv)
        for k in (1, 3, 2):
            used = jnp.where(core == 0, y_targets[k - 1], came)
            send(remote(chunk(n), chunk(n), kv2_ss.at[j + 1, k], kv_rs.at[n], second[k - 1]), used)

    def spread(parts):
        highest = jnp.max(functools.reduce(jnp.maximum, parts), axis=1, keepdims=True)
        return jnp.broadcast_to(highest, parts[0].shape)

    def twice(a):
        return jnp.concatenate([a, a], axis=1)

    def weigh(pieces, new):
        return jnp.concatenate([jnp.exp2((one - new) * SCALE2).astype(BF16) for one in pieces], axis=1)

    def score(h, span, yp, b):
        keys = kt[yp, :, b * BLOCK : (b + 1) * BLOCK]
        both = jnp.dot(qbuf[h, span, :], keys, preferred_element_type=F32)
        return [both[:, n * 128 : (n + 1) * 128] for n in range(BLOCK // 128)]

    def values_of(yp, start, count):
        values = kvbuf[1, pl.ds(pl.multiple_of(yp * SUPER + start, BLOCK), count), :]
        return jnp.concatenate([values, jnp.ones(values.shape, BF16)], axis=1)

    def attend(h, g, yp):
        spans = [pl.ds(pl.multiple_of(g * TILE + t * ROWS, ROWS), ROWS) for t in range(TILE // ROWS)]

        def scores(span):
            return [piece for b in range(SUPER // BLOCK) for piece in score(h, span, yp, b)]

        pieces = scores(spans[0])
        for t, span in enumerate(spans):
            later = scores(spans[t + 1]) if t + 1 < len(spans) else None
            old = top[h, span, :]
            new = jnp.maximum(old, spread(pieces))
            added = jnp.dot(weigh(pieces, new), values_of(yp, 0, SUPER), preferred_element_type=F32)
            acc[h, span, :] = acc[h, span, :] * twice(jnp.exp2((old - new) * SCALE2)) + added
            top[h, span, :] = new
            pieces = later

    def attend_below(h, i, yp, limit):
        span = pl.ds(pl.multiple_of(i * ROWS, ROWS), ROWS)
        lane = lax.broadcasted_iota(jnp.int32, (ROWS, 128), 1)

        def kept(b):
            pieces = score(h, span, yp, b)
            return [
                jnp.where(lane + (b * BLOCK + n * 128) <= limit, one, LOW) for n, one in enumerate(pieces)
            ]

        old, summed = top[h, span, :], acc[h, span, :]
        pieces = kept(0)
        for b in range(SUPER // BLOCK):
            later = kept(b + 1) if b + 1 < SUPER // BLOCK else None
            new = jnp.maximum(old, spread(pieces))
            added = jnp.dot(
                weigh(pieces, new), values_of(yp, b * BLOCK, BLOCK), preferred_element_type=F32
            )
            summed = summed * twice(jnp.exp2((old - new) * SCALE2)) + added
            old, pieces = new, later
        top[h, span, :] = old
        acc[h, span, :] = summed

    def task(h, g, yp):
        yq = jnp.where(h == 0, y, ym)

        @pl.when((yp < yq) | ((yp == yq) & (g > near)))
        def _():
            attend(h, g, yp)

        @pl.when((yp == yq) & (g == near))
        def _():
            edge = lax.div(z, 2)

            def pair(i, _):
                row = lax.broadcasted_iota(jnp.int32, (ROWS, 128), 0)
                here = row + (x * ROWS + h * HALF)
                even = lax.rem(z, 2) == 0
                low = jnp.where(even, here, -1)
                high = jnp.where(even, SUPER, here - HALF)
                limit = jnp.where(row < HALF, low, high)
                attend_below(h, i, yp, jnp.where(i > edge, SUPER, limit))
                return 0

            lax.fori_loop(edge, 2 * g + 2, pair, 0)

    def need_keys(yp):
        for xp in range(X):
            n = yp * X + xp

            @pl.when(jnp.where(core == 0, yp != y, x != xp))
            def _():
                remote(chunk(n), chunk(n), kv1_ss.at[0], kv_rs.at[n], partner).wait_recv()

        for p in range(4):
            rows = pl.ds(pl.multiple_of(yp * SUPER + ROWS * p, ROWS), ROWS)
            kt[yp, :, ROWS * p : ROWS * (p + 1)] = kvbuf[0, rows, :].T

    def need_queries(h, g):
        for t in range(4):
            s = 4 * g + t

            @pl.when(s != z)
            def _():
                r = qbuf.at[h, rows_at(s, HALF)]
                remote(r, r, q_ss.at[0, 0], q_rs.at[h, s], partner).wait_recv()

    def o_copy(h, s):
        where = at(x, jnp.where(h == 0, y, ym), s)
        return remote(obuf.at[h, s], rbuf.at[h, z], o_ss.at[h, s], o_rs.at[h, z], where)

    def finish(h, g):
        def one(t, _):
            s = 4 * g + t
            span = rows_at(s, HALF)
            total = jnp.maximum(acc[h, span, 128:256], TINY)
            obuf[h, s, 0:HALF, :] = (acc[h, span, 0:128] / total).astype(BF16)
            stats = top[h, span, :] * SCALE2 + jnp.log2(total)
            obuf[h, s, HALF:MESSAGE, :] = pack_stats(lane_rows(stats))

            @pl.when((h == 1) | (s != z))
            def _():
                o_copy(h, s).start()

            @pl.when((h == 0) & (s == z))
            def _():
                rbuf[0, z] = obuf[0, z]

            return 0

        lax.fori_loop(0, 4, one, 0)

    count = jnp.maximum(y, ym) + 1

    def superblock(e):
        return jnp.where(e == 0, y, jnp.where(e - 1 >= y, e, e - 1))

    def work(i, _):
        early = i < 4
        n = jnp.where(early, i, i - 4)
        before = jnp.where(y < ym, 0, 1)
        h = jnp.where(early, lax.rem(n, 2), jnp.where(lax.div(n, 2) == 0, before, 1 - before))
        close = jnp.where(early, lax.div(n, 2) == 0, lax.rem(n, 2) == 1)
        g = jnp.where(close, near, 1 - near)

        @pl.when(i == 0)
        def _():
            need_keys(y)

        @pl.when(early)
        def _():
            need_queries(h, g)

        def one(e, _):
            @pl.when(i == 4)
            def _():
                need_keys(superblock(e))

            task(h, g, superblock(e))
            return 0

        lax.fori_loop(jnp.where(early, 0, 1), jnp.where(early, 1, count), one, 0)

        @pl.when(early == ((y == 0) & (h == 0)))
        def _():
            finish(h, g)

        return 0

    lax.fori_loop(0, 8, work, 0)

    def merge(h, _):
        for s in range(Z):

            @pl.when((h == 1) | (z != s))
            def _():
                remote(rbuf.at[h, s], rbuf.at[h, s], o_ss.at[0, 0], o_rs.at[h, s], partner).wait_recv()

        stats = [unpack_stats(rbuf[h, s, HALF:MESSAGE, :]) for s in range(Z)]
        highest = functools.reduce(jnp.maximum, stats)
        shares = [jnp.exp2(one - highest) for one in stats]
        total = functools.reduce(jnp.add, shares)
        merged = jnp.zeros((HALF, HD), F32)
        for s in range(Z):
            merged = merged + rbuf[h, s, 0:HALF, :].astype(F32) * lane_columns(shares[s] / total)
        att[core, rows_at(h, HALF), :] = merged.astype(BF16)
        att_copy(h, core).start()
        return 0

    def att_copy(h, c):
        rows = att.at[c, rows_at(h, HALF)]
        return remote(rows, rows, c_ss.at[1 + h], c_rs.at[1 + h], partner)

    lax.fori_loop(0, 2, merge, 0)

    for condition, copy in sent:
        when(condition, copy.wait_send)

    def drain(s, _):
        for h in range(2):

            @pl.when((h == 1) | (s != z))
            def _():
                o_copy(h, s).wait_send()

        return 0

    lax.fori_loop(0, Z, drain, 0)
    loads[4].wait()
    w_other = w2.at[rows_at(other, HD)]
    remote(w_other, w_other, c_ss.at[0], c_rs.at[0], partner).wait_recv()
    for h in range(2):
        span = slice(h * HALF, (h + 1) * HALF)
        att_copy(h, other).wait_recv()
        both = jnp.concatenate([att[0, span, :], att[1, span, :]], axis=1)
        for n in range(4):
            columns = slice(n * 512, (n + 1) * 512)
            out_ref[span, columns] = jnp.dot(both, w2[:, columns], preferred_element_type=F32).astype(BF16)
    for h in range(2):
        att_copy(h, core).wait_send()


def per_device(queries, keys, values, out_weight):
    hbm = pl.BlockSpec(memory_space=pl.ANY)
    dma = pltpu.SemaphoreType.DMA
    return pl.pallas_call(
        attention_kernel,
        out_shape=pltpu.VMEM((ROWS, WIDTH), BF16),
        in_specs=[hbm] * 4,
        out_specs=pl.BlockSpec(memory_space=pltpu.VMEM),
        scratch_shapes=[
            pltpu.VMEM((2, LINE, HD), BF16),
            pltpu.VMEM((2, Y * SUPER, HD), BF16),
            pltpu.VMEM((Y, HD, SUPER), BF16),
            pltpu.VMEM((HALF, HD), BF16),
            pltpu.VMEM((2, LINE, 256), F32),
            pltpu.VMEM((2, LINE, 128), F32),
            pltpu.VMEM((2, Z, MESSAGE, HD), BF16),
            pltpu.VMEM((2, Z, MESSAGE, HD), BF16),
            pltpu.VMEM((2, ROWS, HD), BF16),
            pltpu.VMEM((2 * HD, WIDTH), BF16),
            dma((5,)), dma((4,)), dma((4, 4)), dma((16,)), dma, dma((2, 8)), dma((2, 8)), dma((2, 8)), dma((2, 8)),
            dma((3,)), dma((3,)),
        ],
        compiler_params=pltpu.CompilerParams(
            collective_id=0, has_side_effects=True, vmem_limit_bytes=56 << 20
        ),
    )(queries[0], keys[0], values[0], out_weight[0])


def solution(mesh):
    placed = (
        P("head", "ctx", None),
        P("head", "ctx", None),
        P("head", "ctx", None),
        P("head", None, None),
    )
    return jax.shard_map(
        per_device, mesh=mesh, in_specs=placed, out_specs=P("ctx", "head"), check_vma=False
    )
```

```python
import functools
import math

import jax
import jax.numpy as jnp
from jax import lax
from jax.experimental import pallas as pl
from jax.experimental.pallas import tpu as pltpu
from jax.sharding import PartitionSpec as P

MESH = pl.DeviceIdType.MESH
X, Y, Z = 4, 4, 8
ROWS = 384
HALF = ROWS // 2
HD = 128
LINE = Z * HALF
SUPER = X * ROWS
TILE = LINE // 2
BLOCK = 512
PART = 256
WIDTH = 2048
MESSAGE = HALF + 16
SCALE2 = math.log2(math.e) / math.sqrt(HD)
LOW = -1e30
TINY = 1e-30
BF16, F32 = jnp.bfloat16, jnp.float32


def lane_rows(columns):
    return jnp.concatenate([columns[0:128].T[0:1], columns[HALF - 128 : HALF].T[0:1]], axis=0)


def lane_columns(rows):
    low = jnp.broadcast_to(rows[0:1], (128, 128)).T
    high = jnp.broadcast_to(rows[1:2], (128, 128)).T
    return jnp.concatenate([low, high[256 - HALF : 128]], axis=0)


def pack_stats(rows):
    high = rows.astype(BF16).astype(F32)
    mid = (rows - high).astype(BF16).astype(F32)
    low = rows - high - mid
    return jnp.concatenate([high, mid, low, jnp.zeros((10, 128), F32)], axis=0).astype(BF16)


def unpack_stats(packed):
    wide = packed.astype(F32)
    return wide[0:2] + wide[2:4] + wide[4:6]


def attention_kernel(
    q_ref, k_ref, v_ref, w_ref, out_ref,
    qbuf, kvbuf, kt, swap, acc, top, obuf, rbuf, att, w2,
    in_s, kv1_ss, kv2_ss, kv_rs, swap_ss, q_ss, q_rs, o_ss, o_rs, c_ss, c_rs,
):
    index, core = lax.axis_index("ctx"), lax.axis_index("head")
    x, z, y = lax.rem(index, X), lax.rem(lax.div(index, X), Z), lax.div(index, X * Z)
    ym = Y - 1 - y
    near = lax.div(z, 4)

    def at(px, py, pz, pc=None):
        return ((py * Z + pz) * X + px, core if pc is None else pc)

    def ring(p, d, n):
        return lax.rem(p + d + n, n)

    def remote(src, dst, ss, rs, where):
        return pltpu.make_async_remote_copy(
            src_ref=src, dst_ref=dst, send_sem=ss, recv_sem=rs, device_id=where, device_id_type=MESH
        )

    other = 1 - core
    partner = at(x, y, z, other)
    x_peers = [at(ring(x, k, X), y, z) for k in range(1, X)]
    y_peers = [at(x, ring(y, k, Y), z) for k in range(1, Y)]
    lines = [[at(x, yy, ring(z, k, Z)) for k in range(Z)] for yy in (y, ym)]
    first = [(jnp.where(core == 0, a[0], b[0]), core) for a, b in zip(x_peers, y_peers)]
    second = [(jnp.where(core == 0, b[0], a[0]), core) for a, b in zip(x_peers, y_peers)]

    def rows_at(n, size):
        return pl.ds(pl.multiple_of(n * size, size), size)

    def chunk(n):
        return kvbuf.at[:, rows_at(n, ROWS), :]

    mine = y * X + x
    loads = [
        pltpu.make_async_copy(k_ref, kvbuf.at[0, rows_at(mine, ROWS)], in_s.at[0]),
        pltpu.make_async_copy(v_ref, kvbuf.at[1, rows_at(mine, ROWS)], in_s.at[1]),
        pltpu.make_async_copy(q_ref.at[0:HALF], qbuf.at[0, rows_at(z, HALF)], in_s.at[2]),
        pltpu.make_async_copy(q_ref.at[HALF:ROWS], swap, in_s.at[3]),
        pltpu.make_async_copy(
            w_ref.at[:, rows_at(core, WIDTH)], w2.at[rows_at(core, HD)], in_s.at[4]
        ),
    ]
    for copy in loads:
        copy.start()

    barrier = pltpu.get_barrier_semaphore()
    for where in lines[0][1:] + lines[1] + x_peers + y_peers + [partner]:
        pl.semaphore_signal(barrier, inc=1, device_id=where, device_id_type=MESH)
    pl.semaphore_wait(barrier, 22)

    sent = []

    def when(condition, act):
        if condition is None:
            act()
        else:
            pl.when(condition)(act)

    def send(copy, condition=None):
        when(condition, copy.start)
        sent.append((condition, copy))

    def needed(source, target):
        return (source <= target) | (source <= Y - 1 - target)

    y_targets = [needed(y, ring(y, k, Y)) for k in range(1, Y)]

    for copy in loads[:4]:
        copy.wait()
    for k in (1, 3, 2):
        used = (core == 0) | y_targets[k - 1]
        send(remote(chunk(mine), chunk(mine), kv1_ss.at[k], kv_rs.at[mine], first[k - 1]), used)
    own_rows = [qbuf.at[h, rows_at(z, HALF)] for h in range(2)]
    send(remote(swap, own_rows[1], swap_ss, q_rs.at[1, z], lines[1][0]))
    for k in (1, 7, 2, 6, 3, 5, 4):
        send(remote(own_rows[0], own_rows[0], q_ss.at[0, k], q_rs.at[0, z], lines[0][k]))
    remote(own_rows[1], own_rows[1], swap_ss, q_rs.at[1, z], partner).wait_recv()
    for k in (1, 7, 2, 6, 3, 5, 4):
        send(remote(own_rows[1], own_rows[1], q_ss.at[1, k], q_rs.at[1, z], lines[0][k]))
    for k in (1, 3, 2):
        used = (core == 1) | y_targets[k - 1]
        send(remote(chunk(mine), chunk(mine), kv2_ss.at[0, k], kv_rs.at[mine], second[k - 1]), used)
    send(
        remote(
            w_ref.at[:, rows_at(other, WIDTH)], w2.at[rows_at(core, HD)], c_ss.at[0], c_rs.at[0], partner
        )
    )

    def clear(n, _):
        acc[n] = jnp.zeros((LINE, 256), F32)
        top[n] = jnp.full((LINE, 128), LOW, F32)
        return 0

    lax.fori_loop(0, 2, clear, 0)

    for j, k in enumerate((1, 3, 2)):
        source = jnp.where(jnp.int32(j) >= y, j + 1, j)
        n = jnp.where(core == 0, y * X + ring(x, -k, X), source * X + x)
        came = (core == 0) | needed(source, y)
        when(came, remote(chunk(n), chunk(n), kv1_ss.at[j], kv_rs.at[n], partner).wait_recv)
        for k in (1, 3, 2):
            used = jnp.where(core == 0, y_targets[k - 1], came)
            send(remote(chunk(n), chunk(n), kv2_ss.at[j + 1, k], kv_rs.at[n], second[k - 1]), used)

    def spread(parts):
        highest = jnp.max(functools.reduce(jnp.maximum, parts), axis=1, keepdims=True)
        return jnp.broadcast_to(highest, parts[0].shape)

    def twice(a):
        return jnp.concatenate([a, a], axis=1)

    def weigh(pieces, new):
        return jnp.concatenate([jnp.exp2((one - new) * SCALE2).astype(BF16) for one in pieces], axis=1)

    def score(h, span, yp, b):
        keys = kt[yp, :, b * BLOCK : (b + 1) * BLOCK]
        both = jnp.dot(qbuf[h, span, :], keys, preferred_element_type=F32)
        return [both[:, n * 128 : (n + 1) * 128] for n in range(BLOCK // 128)]

    def values_of(yp, start, count):
        values = kvbuf[1, pl.ds(pl.multiple_of(yp * SUPER + start, BLOCK), count), :]
        return jnp.concatenate([values, jnp.ones(values.shape, BF16)], axis=1)

    def attend(h, g, yp):
        spans = [pl.ds(pl.multiple_of(g * TILE + t * PART, PART), PART) for t in range(TILE // PART)]

        def scores(span):
            return [piece for b in range(SUPER // BLOCK) for piece in score(h, span, yp, b)]

        pieces = scores(spans[0])
        for t, span in enumerate(spans):
            later = scores(spans[t + 1]) if t + 1 < len(spans) else None
            old = top[h, span, :]
            new = jnp.maximum(old, spread(pieces))
            added = jnp.dot(weigh(pieces, new), values_of(yp, 0, SUPER), preferred_element_type=F32)
            acc[h, span, :] = acc[h, span, :] * twice(jnp.exp2((old - new) * SCALE2)) + added
            top[h, span, :] = new
            pieces = later

    def attend_below(h, i, yp, limit):
        span = pl.ds(pl.multiple_of(i * ROWS, ROWS), ROWS)
        lane = lax.broadcasted_iota(jnp.int32, (ROWS, 128), 1)

        def kept(b):
            pieces = score(h, span, yp, b)
            return [
                jnp.where(lane + (b * BLOCK + n * 128) <= limit, one, LOW) for n, one in enumerate(pieces)
            ]

        old, summed = top[h, span, :], acc[h, span, :]
        pieces = kept(0)
        for b in range(SUPER // BLOCK):
            later = kept(b + 1) if b + 1 < SUPER // BLOCK else None
            new = jnp.maximum(old, spread(pieces))
            added = jnp.dot(
                weigh(pieces, new), values_of(yp, b * BLOCK, BLOCK), preferred_element_type=F32
            )
            summed = summed * twice(jnp.exp2((old - new) * SCALE2)) + added
            old, pieces = new, later
        top[h, span, :] = old
        acc[h, span, :] = summed

    def task(h, g, yp):
        yq = jnp.where(h == 0, y, ym)

        @pl.when((yp < yq) | ((yp == yq) & (g > near)))
        def _():
            attend(h, g, yp)

        @pl.when((yp == yq) & (g == near))
        def _():
            edge = lax.div(z, 2)

            def pair(i, _):
                row = lax.broadcasted_iota(jnp.int32, (ROWS, 128), 0)
                here = row + (x * ROWS + h * HALF)
                even = lax.rem(z, 2) == 0
                low = jnp.where(even, here, -1)
                high = jnp.where(even, SUPER, here - HALF)
                limit = jnp.where(row < HALF, low, high)
                attend_below(h, i, yp, jnp.where(i > edge, SUPER, limit))
                return 0

            lax.fori_loop(edge, 2 * g + 2, pair, 0)

    def need_keys(yp):
        for xp in range(X):
            n = yp * X + xp

            @pl.when(jnp.where(core == 0, yp != y, x != xp))
            def _():
                remote(chunk(n), chunk(n), kv1_ss.at[0], kv_rs.at[n], partner).wait_recv()

        for p in range(4):
            rows = pl.ds(pl.multiple_of(yp * SUPER + ROWS * p, ROWS), ROWS)
            kt[yp, :, ROWS * p : ROWS * (p + 1)] = kvbuf[0, rows, :].T

    def need_queries(h, g):
        for t in range(4):
            s = 4 * g + t

            @pl.when(s != z)
            def _():
                r = qbuf.at[h, rows_at(s, HALF)]
                remote(r, r, q_ss.at[0, 0], q_rs.at[h, s], partner).wait_recv()

    def o_copy(h, s):
        where = at(x, jnp.where(h == 0, y, ym), s)
        return remote(obuf.at[h, s], rbuf.at[h, z], o_ss.at[h, s], o_rs.at[h, z], where)

    def finish(h, g):
        def one(t, _):
            s = 4 * g + t
            span = rows_at(s, HALF)
            total = jnp.maximum(acc[h, span, 128:256], TINY)
            obuf[h, s, 0:HALF, :] = (acc[h, span, 0:128] / total).astype(BF16)
            stats = top[h, span, :] * SCALE2 + jnp.log2(total)
            obuf[h, s, HALF:MESSAGE, :] = pack_stats(lane_rows(stats))

            @pl.when((h == 1) | (s != z))
            def _():
                o_copy(h, s).start()

            @pl.when((h == 0) & (s == z))
            def _():
                rbuf[0, z] = obuf[0, z]

            return 0

        lax.fori_loop(0, 4, one, 0)

    count = jnp.maximum(y, ym) + 1

    def superblock(e):
        return jnp.where(e == 0, y, jnp.where(e - 1 >= y, e, e - 1))

    def work(i, _):
        early = i < 4
        n = jnp.where(early, i, i - 4)
        before = jnp.where(y < ym, 0, 1)
        h = jnp.where(early, lax.rem(n, 2), jnp.where(lax.div(n, 2) == 0, before, 1 - before))
        close = jnp.where(early, lax.div(n, 2) == 0, lax.rem(n, 2) == 1)
        g = jnp.where(close, near, 1 - near)

        @pl.when(i == 0)
        def _():
            need_keys(y)

        @pl.when(early)
        def _():
            need_queries(h, g)

        def one(e, _):
            @pl.when(i == 4)
            def _():
                need_keys(superblock(e))

            task(h, g, superblock(e))
            return 0

        lax.fori_loop(jnp.where(early, 0, 1), jnp.where(early, 1, count), one, 0)

        @pl.when(early == ((y == 0) & (h == 0)))
        def _():
            finish(h, g)

        return 0

    lax.fori_loop(0, 8, work, 0)

    def merge(h, _):
        for s in range(Z):

            @pl.when((h == 1) | (z != s))
            def _():
                remote(rbuf.at[h, s], rbuf.at[h, s], o_ss.at[0, 0], o_rs.at[h, s], partner).wait_recv()

        stats = [unpack_stats(rbuf[h, s, HALF:MESSAGE, :]) for s in range(Z)]
        highest = functools.reduce(jnp.maximum, stats)
        shares = [jnp.exp2(one - highest) for one in stats]
        total = functools.reduce(jnp.add, shares)
        merged = jnp.zeros((HALF, HD), F32)
        for s in range(Z):
            merged = merged + rbuf[h, s, 0:HALF, :].astype(F32) * lane_columns(shares[s] / total)
        att[core, rows_at(h, HALF), :] = merged.astype(BF16)
        att_copy(h, core).start()
        return 0

    def att_copy(h, c):
        rows = att.at[c, rows_at(h, HALF)]
        return remote(rows, rows, c_ss.at[1 + h], c_rs.at[1 + h], partner)

    lax.fori_loop(0, 2, merge, 0)

    for condition, copy in sent:
        when(condition, copy.wait_send)

    def drain(s, _):
        for h in range(2):

            @pl.when((h == 1) | (s != z))
            def _():
                o_copy(h, s).wait_send()

        return 0

    lax.fori_loop(0, Z, drain, 0)
    loads[4].wait()
    w_other = w2.at[rows_at(other, HD)]
    remote(w_other, w_other, c_ss.at[0], c_rs.at[0], partner).wait_recv()
    for h in range(2):
        span = slice(h * HALF, (h + 1) * HALF)
        att_copy(h, other).wait_recv()
        both = jnp.concatenate([att[0, span, :], att[1, span, :]], axis=1)
        for n in range(4):
            columns = slice(n * 512, (n + 1) * 512)
            out_ref[span, columns] = jnp.dot(both, w2[:, columns], preferred_element_type=F32).astype(BF16)
    for h in range(2):
        att_copy(h, core).wait_send()


def per_device(queries, keys, values, out_weight):
    hbm = pl.BlockSpec(memory_space=pl.ANY)
    dma = pltpu.SemaphoreType.DMA
    return pl.pallas_call(
        attention_kernel,
        out_shape=pltpu.VMEM((ROWS, WIDTH), BF16),
        in_specs=[hbm] * 4,
        out_specs=pl.BlockSpec(memory_space=pltpu.VMEM),
        scratch_shapes=[
            pltpu.VMEM((2, LINE, HD), BF16),
            pltpu.VMEM((2, Y * SUPER, HD), BF16),
            pltpu.VMEM((Y, HD, SUPER), BF16),
            pltpu.VMEM((HALF, HD), BF16),
            pltpu.VMEM((2, LINE, 256), F32),
            pltpu.VMEM((2, LINE, 128), F32),
            pltpu.VMEM((2, Z, MESSAGE, HD), BF16),
            pltpu.VMEM((2, Z, MESSAGE, HD), BF16),
            pltpu.VMEM((2, ROWS, HD), BF16),
            pltpu.VMEM((2 * HD, WIDTH), BF16),
            dma((5,)), dma((4,)), dma((4, 4)), dma((16,)), dma, dma((2, 8)), dma((2, 8)), dma((2, 8)), dma((2, 8)),
            dma((3,)), dma((3,)),
        ],
        compiler_params=pltpu.CompilerParams(
            collective_id=0, has_side_effects=True, vmem_limit_bytes=56 << 20
        ),
    )(queries[0], keys[0], values[0], out_weight[0])


def solution(mesh):
    placed = (
        P("head", "ctx", None),
        P("head", "ctx", None),
        P("head", "ctx", None),
        P("head", None, None),
    )
    return jax.shard_map(
        per_device, mesh=mesh, in_specs=placed, out_specs=P("ctx", "head"), check_vma=False
    )
```
